256 devices in a mesh: sec: 2 (over z_hi), grp: 16 (over x, z_lo), tp: 8 (over y, core).
Axes of the slice: x: 4, y: 4, z: 8 (z_hi: 2, z_lo: 4; z = z_hi * 4 + z_lo), core: 2. Of those that a mesh axis runs over, the one named last changes fastest.
Arguments:
- pre_query: bfloat16 [32, 1024, 8192], P(('sec', 'grp'), 'tp'), may hold values from -6 to 6
- pre_keys: bfloat16 [32, 2048, 1024], P(('sec', 'grp'), 'tp'), may hold values from -6 to 6
- pre_values: bfloat16 [32, 2048, 1024], P(('sec', 'grp'), 'tp'), may hold values from -6 to 6
- dec_query: bfloat16 [32, 2, 64, 8192], P(('sec', 'grp'), None, None, 'tp'), may hold values from -6 to 6
- dec_new_keys: bfloat16 [32, 2, 64, 1024], P(('sec', 'grp'), None, None, 'tp'), may hold values from -6 to 6
- dec_new_values: bfloat16 [32, 2, 64, 1024], P(('sec', 'grp'), None, None, 'tp'), may hold values from -6 to 6
- cache_keys: bfloat16 [32, 64, 16, 1024], P(('sec', 'grp'), None, None, 'tp'), may hold values from -6 to 6
- cache_values: bfloat16 [32, 64, 16, 1024], P(('sec', 'grp'), None, None, 'tp'), may hold values from -6 to 6
- cache_lens: int32 [32, 64], P(('sec', 'grp')), may hold values from 1 to 16
- pool_keys: bfloat16 [32, 8, 32, 16, 1024], P(('sec', 'grp'), 'tp'), may hold values from -6 to 6
- pool_values: bfloat16 [32, 8, 32, 16, 1024], P(('sec', 'grp'), 'tp'), may hold values from -6 to 6
- block_owner: int32 [32, 8, 32, 1], P(('sec', 'grp'), 'tp'), may hold values from 0 to 31; in each aligned block of 32 rows (0 to 31, 32 to 63, ..., all dimensions but the last counted through in order) at most 2 rows name the same one
- block_count: int32 [32, 8, 32], P(('sec', 'grp'), 'tp'), may hold values from 1 to 16
Outputs:
- pre_out: bfloat16 [32, 1024, 8192], P(('sec', 'grp'), 'tp')
- dec_out: bfloat16 [32, 2, 64, 8192], P(('sec', 'grp'), None, None, 'tp')
- pages_keys: bfloat16 [32, 32, 8, 2, 16, 1024], P(('sec', 'grp'), None, None, None, None, 'tp')
- pages_values: bfloat16 [32, 32, 8, 2, 16, 1024], P(('sec', 'grp'), None, None, None, None, 'tp')
The draws below stay inside these ranges and needn't reach their ends.
Inputs may be any that keep to these rules, and one draw needn't show every extreme that they name: `block_owner`: no owner is named by more than 2 of the blocks of one device, and some device names some owner exactly 2 times.
All inputs are finite; a program needn't handle non-finite values.
Results may differ from the reference program's by a relative error of at most 0.0085.
Values may be sent and summed in bfloat16 or wider, within the bound.
A program may use at most 192 MiB of HBM per device.

```python
import math
import jax
import jax.numpy as jnp
import numpy as np
from jax import lax

H = 64
KVH = 8
HD = 128
G = 8
ROWS = 64
CACHE = 16
DSTEPS = 2
BLOCK = 16
CAP = 2
R = 32
SPAN = 1024
KEYS = 2048
PRIOR = 1024
POOL_DEV = 32
N_TP = 8


def draw_pre_query(key, part):
    key = jax.random.fold_in(key, 11)
    base_key = jax.random.fold_in(key, 0)
    values = jnp.clip(jax.random.normal(base_key, (R, SPAN, H * HD), jnp.float32), -6.0, 6.0)
    return values.astype(jnp.bfloat16)


def draw_pre_keys(key, part):
    key = jax.random.fold_in(key, 12)
    base_key = jax.random.fold_in(key, 0)
    values = jnp.clip(jax.random.normal(base_key, (R, KEYS, KVH * HD), jnp.float32), -6.0, 6.0)
    return values.astype(jnp.bfloat16)


def draw_dec_query(key, part):
    key = jax.random.fold_in(key, 13)
    base_key = jax.random.fold_in(key, 0)
    values = jnp.clip(jax.random.normal(base_key, (R, DSTEPS, ROWS, H * HD), jnp.float32), -6.0, 6.0)
    return values.astype(jnp.bfloat16)


def draw_cache_keys(key, part):
    key = jax.random.fold_in(key, 14)
    base_key = jax.random.fold_in(key, 0)
    values = jnp.clip(jax.random.normal(base_key, (R, ROWS, CACHE, KVH * HD), jnp.float32), -6.0, 6.0)
    return values.astype(jnp.bfloat16)


def place_ends(drawn, rng, smallest, top_value):
    longest = drawn.shape.index(max(drawn.shape))
    spots = []
    for shift in (0, 1):
        where = [jax.random.randint(jax.random.fold_in(rng, axis), (), 0, length) for axis, length in enumerate(drawn.shape)]
        where[longest] = (where[longest] + shift) % drawn.shape[longest]
        spots.append(tuple(where))
    return drawn.at[spots[0]].set(smallest).at[spots[1]].set(top_value)


def level_of(key, shape, cuts, least, high):
    level = 1.0
    for position, parts in cuts:
        draws = jax.random.uniform(jax.random.fold_in(jax.random.fold_in(key, 6), position), (parts,), jnp.float32, least / len(cuts), high / len(cuts))
        level = level * jnp.repeat(jnp.exp(draws), shape[position] // parts).reshape((-1,) + (1,) * (len(shape) - 1 - position))
    return level


def routed_block(own_key, own, number, rows, number_of, top, bound, slope):
    order = jax.random.permutation(own_key, number_of)
    crowded, common = portions_of(number_of, rows * top, bound, slope, True), portions_of(number_of, rows * top, bound, slope, False)
    places = jnp.arange(number_of)

    def named(tallies, turn):
        used = int((tallies > 0).sum())
        fixed = max(1, used // 4)
        moved = fixed + (places - fixed + turn * (used - fixed)) % max(1, number_of - fixed)
        return jnp.zeros((number_of,), jnp.int32).at[order[jnp.where(places < fixed, places, moved)]].set(jnp.asarray(tallies, jnp.int32))

    tallies = jnp.where(number % 4 == 0, named(crowded, number // 4), named(common, number - number // 4 - 1))
    mixed = jax.random.permutation(jax.random.fold_in(own, 3), number_of)
    source_of, receiver = mixed[0:number_of // 2 * 2:2], mixed[1:number_of // 2 * 2:2]
    margin = jnp.minimum(tallies[source_of] - 1, bound - tallies[receiver]) // 2
    margin = jnp.where((source_of == order[0]) | (receiver == order[0]) | (tallies[receiver] == 0), 0, jnp.maximum(margin, 0))
    moved = jax.random.randint(jax.random.fold_in(own, 4), (number_of // 2,), 0, 1 << 20) % (margin + 1)
    tallies = tallies.at[source_of].add(-moved).at[receiver].add(moved)
    items = jnp.searchsorted(jnp.cumsum(tallies), jnp.arange(rows * top), side="right").astype(jnp.int32)
    table = items.reshape(top, rows).T
    table = table[jax.random.permutation(jax.random.fold_in(own, 1), rows)]
    turn = jax.random.randint(jax.random.fold_in(own, 2), (rows, 1), 0, top)
    return jnp.take_along_axis(table, (jnp.arange(top)[None, :] + turn) % top, axis=1)


def portions_of(count, total, reach, slope, full):
    portions = [(1 << 20) // math.isqrt(rank ** slope) + 1 for rank in range(1, count + 1)]
    largest = reach if full else min(reach, max(-(-total // count), total * portions[0] // sum(portions)))
    least = 1 if total - largest >= count - 1 else 0
    given, surplus = [largest] + [least] * (count - 1), total - largest - least * (count - 1)
    while surplus > 0:
        candidates = [i for i in range(1, count) if given[i] < largest] or [i for i in range(1, count) if given[i] < reach]
        mass, budget = sum([portions[i] for i in candidates]), surplus
        for i in candidates:
            more = min(reach - given[i], max(1, budget * portions[i] // mass), surplus)
            given[i] = given[i] + more
            surplus = surplus - more
    return np.array(given)


def normal_values(own_key, shape, deviation, reach, cuts=(), kind=jnp.bfloat16):
    drawn = deviation * jax.random.normal(own_key, shape, jnp.float32)
    if cuts:
        drawn = drawn * level_of(own_key, shape, cuts, -0.22, 0.18)
    return jnp.clip(drawn, -reach, reach).astype(kind)


def setup_inputs(seed: int = 0) -> dict:
    key_of = jax.random.split(jax.random.key(seed), 14)
    pre_query = draw_pre_query(jax.random.fold_in(key_of[13], 71), 0)
    pre_keys = draw_pre_keys(jax.random.fold_in(key_of[13], 71), 0)
    pre_values = normal_values(key_of[2], (R, KEYS, KVH * HD), 1.0, 6.0, ((0, 32), (1, 8)))
    dec_query = draw_dec_query(jax.random.fold_in(key_of[13], 71), 0)
    dec_new_keys = normal_values(key_of[4], (R, DSTEPS, ROWS, KVH * HD), 1.0, 6.0, ((0, 32), (3, 8)))
    dec_new_values = normal_values(key_of[5], (R, DSTEPS, ROWS, KVH * HD), 1.0, 6.0, ((0, 32), (3, 8)))
    cache_keys = draw_cache_keys(jax.random.fold_in(key_of[13], 71), 0)
    cache_values = normal_values(key_of[7], (R, ROWS, CACHE, KVH * HD), 1.0, 6.0, ((0, 32), (3, 8)))
    cache_lens = place_ends(jax.random.randint(key_of[8], (R, ROWS), 1, CACHE + 1), jax.random.fold_in(key_of[8], 1), 1, CACHE).astype(jnp.int32)
    pool_keys = normal_values(key_of[9], (R, N_TP, POOL_DEV, BLOCK, KVH * HD), 1.0, 6.0, ((0, 32), (1, 8)))
    pool_values = normal_values(key_of[10], (R, N_TP, POOL_DEV, BLOCK, KVH * HD), 1.0, 6.0, ((0, 32), (1, 8)))
    block_owner_keys = jax.random.split(jax.random.fold_in(key_of[11], 1), R * N_TP * POOL_DEV // POOL_DEV)
    block_owner_turns = jax.random.permutation(jax.random.fold_in(key_of[11], 3), R * N_TP * POOL_DEV // POOL_DEV)
    block_owner = jax.vmap(lambda own, number: routed_block(jax.random.fold_in(key_of[11], 2), own, number, POOL_DEV, R, 1, CAP, 2))(block_owner_keys, block_owner_turns).reshape((R, N_TP, POOL_DEV, 1))
    block_count = place_ends(jax.random.randint(key_of[12], (R, N_TP, POOL_DEV), 1, BLOCK + 1), jax.random.fold_in(key_of[12], 1), 1, BLOCK).astype(jnp.int32)
    return {"pre_query": pre_query, "pre_keys": pre_keys, "pre_values": pre_values, "dec_query": dec_query, "dec_new_keys": dec_new_keys, "dec_new_values": dec_new_values, "cache_keys": cache_keys, "cache_values": cache_values, "cache_lens": cache_lens, "pool_keys": pool_keys, "pool_values": pool_values, "block_owner": block_owner, "block_count": block_count}


MASKED_SCORE = -1e30


def prefill_head(operands, allowed):
    queries, key_rows, value_rows = operands
    scores = jnp.einsum("qgd,td->qgt", queries, key_rows) * (HD ** -0.5)
    scores = jnp.where(allowed[:, None, :], scores, MASKED_SCORE)
    row_max = jnp.max(scores, axis=-1, keepdims=True)
    weights = jnp.where(allowed[:, None, :], jnp.exp(scores - row_max), 0.0)
    denominator = jnp.sum(weights, axis=-1)
    rounded = lax.optimization_barrier(weights.astype(jnp.bfloat16)).astype(jnp.float32)
    mixture = jnp.einsum("qgt,td->qgd", rounded, value_rows)
    return mixture / denominator[..., None]


def prefill_prompt(operands):
    queries, key_rows, value_rows = operands
    query_pos = PRIOR + jnp.arange(SPAN, dtype=jnp.int32)
    key_pos = jnp.arange(KEYS, dtype=jnp.int32)
    allowed = key_pos[None, :] <= query_pos[:, None]
    grouped = jnp.transpose(queries.astype(jnp.float32).reshape(SPAN, KVH, G, HD), (1, 0, 2, 3))
    key_heads = jnp.transpose(key_rows.astype(jnp.float32).reshape(KEYS, KVH, HD), (1, 0, 2))
    value_heads = jnp.transpose(value_rows.astype(jnp.float32).reshape(KEYS, KVH, HD), (1, 0, 2))
    mixture = lax.map(lambda triple: prefill_head(triple, allowed), (grouped, key_heads, value_heads))
    return jnp.transpose(mixture, (1, 0, 2, 3)).reshape(SPAN, H * HD).astype(jnp.bfloat16)


def decode_replica(operands):
    queries, new_keys, new_values, resident_keys, resident_values, lengths = operands
    scaling = HD ** -0.5
    grouped = queries.astype(jnp.float32).reshape(DSTEPS, ROWS, KVH, G, HD)
    cache_k = resident_keys.astype(jnp.float32).reshape(ROWS, CACHE, KVH, HD)
    cache_v = resident_values.astype(jnp.float32).reshape(ROWS, CACHE, KVH, HD)
    fresh_k = new_keys.astype(jnp.float32).reshape(DSTEPS, ROWS, KVH, HD)
    fresh_v = new_values.astype(jnp.float32).reshape(DSTEPS, ROWS, KVH, HD)
    cache_scores = jnp.einsum("sbkgd,bckd->sbkgc", grouped, cache_k) * scaling
    fresh_scores = jnp.einsum("sbkgd,ubkd->sbkgu", grouped, fresh_k) * scaling
    cache_ok = (jnp.arange(CACHE, dtype=jnp.int32)[None, :] < lengths[:, None])[None, :, None, None, :]
    fresh_ok = (jnp.arange(DSTEPS, dtype=jnp.int32)[None, :] <= jnp.arange(DSTEPS, dtype=jnp.int32)[:, None])[:, None, None, None, :]
    cache_scores = jnp.where(cache_ok, cache_scores, MASKED_SCORE)
    fresh_scores = jnp.where(fresh_ok, fresh_scores, MASKED_SCORE)
    row_max = jnp.maximum(jnp.max(cache_scores, axis=-1), jnp.max(fresh_scores, axis=-1))[..., None]
    cache_weights = jnp.where(cache_ok, jnp.exp(cache_scores - row_max), 0.0)
    fresh_weights = jnp.where(fresh_ok, jnp.exp(fresh_scores - row_max), 0.0)
    denominator = jnp.sum(cache_weights, axis=-1) + jnp.sum(fresh_weights, axis=-1)
    cache_round = lax.optimization_barrier(cache_weights.astype(jnp.bfloat16)).astype(jnp.float32)
    fresh_round = lax.optimization_barrier(fresh_weights.astype(jnp.bfloat16)).astype(jnp.float32)
    mixture = jnp.einsum("sbkgc,bckd->sbkgd", cache_round, cache_v) + jnp.einsum("sbkgu,ubkd->sbkgd", fresh_round, fresh_v)
    return (mixture / denominator[..., None]).reshape(DSTEPS, ROWS, H * HD).astype(jnp.bfloat16)


def hand_blocks(pool, owners, counts):
    usable = jnp.arange(BLOCK, dtype=jnp.int32)[None, None, None, :] < counts[..., None]
    masked = jnp.where(usable[..., None], pool, jnp.zeros((), pool.dtype))
    destination = owners[..., 0]
    onehot = (destination[..., None] == jnp.arange(R, dtype=jnp.int32)[None, None, None, :]).astype(jnp.int32)
    slot_index = jnp.sum((jnp.cumsum(onehot, axis=2).astype(jnp.int32) - 1) * onehot, axis=-1).astype(jnp.int32)
    source_rep = jnp.broadcast_to(jnp.arange(R, dtype=jnp.int32)[:, None, None], destination.shape)
    source_dev = jnp.broadcast_to(jnp.arange(N_TP, dtype=jnp.int32)[None, :, None], destination.shape)
    pages = jnp.zeros((R, R, N_TP, CAP, BLOCK, KVH * HD), pool.dtype)
    return pages.at[destination, source_rep, source_dev, slot_index].set(masked)


def reference(pre_query, pre_keys, pre_values, dec_query, dec_new_keys, dec_new_values, cache_keys, cache_values, cache_lens, pool_keys, pool_values, block_owner, block_count):
    pre_out = lax.map(prefill_prompt, (pre_query, pre_keys, pre_values))
    dec_out = lax.map(decode_replica, (dec_query, dec_new_keys, dec_new_values, cache_keys, cache_values, cache_lens))
    pages_keys = hand_blocks(pool_keys, block_owner, block_count)
    pages_values = hand_blocks(pool_values, block_owner, block_count)
    return (pre_out, dec_out, pages_keys, pages_values)
```

```python
import jax
import jax.numpy as jnp
from jax import lax
from jax.experimental import pallas as pl
from jax.experimental.pallas import tpu as pltpu
from jax.sharding import PartitionSpec as P

H = 64
KVH = 8
HD = 128
G = 8
CAP = 2
BLOCK = 16
REPS = 32
NTP = 8
SPAN_DEV = 128
KEY_DEV = 256
CHIP_KEYS = 2 * KEY_DEV
PRIOR = 1024
ROWS = 64
STEPS = 2
CACHE = 16
UNITS = REPS * NTP
ROW_TILE = 256
LOG2E_SCALE = 1.4426950408889634 * HD**-0.5
MASKED = -1e30
MESH = pl.DeviceIdType.MESH


def position():
    sec, grp, tp = lax.axis_index("sec"), lax.axis_index("grp"), lax.axis_index("tp")
    return grp // 4, tp // 2, sec * 4 + lax.rem(grp, 4), lax.rem(tp, 2)


def replica_at(x, z):
    return z // 4, x * 4 + lax.rem(z, 4)


def kernel(
    table,
    lens,
    pre_q,
    pre_k,
    pre_v,
    dec_q,
    new_k,
    new_v,
    cache_k,
    cache_v,
    pool_k,
    pool_v,
    pre_out,
    dec_out,
    pages,
    qbuf,
    kbuf,
    vbuf,
    poolbuf,
    sendbuf,
    top,
    total,
    accum,
    obuf,
    dqbuf,
    nbuf,
    cbuf,
    dobuf,
    ready,
    load_sem,
    own_sem,
    kv_send,
    kv_relay,
    kv_recv,
    page_send,
    page_recv,
    store_sem,
):
    x, y, z, core = position()
    sec, grp, tp = lax.axis_index("sec"), lax.axis_index("grp"), lax.axis_index("tp")
    me = (sec * 16 + grp) * NTP + tp
    other = y * 2 + 1 - core

    def shifted(k):
        return replica_at(lax.rem(x + k // 8, 4), lax.rem(z + lax.rem(k, 8), 8))

    def sibling(k):
        return lax.rem(tp + k, NTP)

    loads = [
        pltpu.make_async_copy(pool_k.at[0, 0], poolbuf.at[0], load_sem.at[0]),
        pltpu.make_async_copy(pool_v.at[0, 0], poolbuf.at[1], load_sem.at[1]),
        pltpu.make_async_copy(dec_q.at[0], dqbuf, load_sem.at[2]),
        pltpu.make_async_copy(new_k.at[0], nbuf.at[0], load_sem.at[3]),
        pltpu.make_async_copy(new_v.at[0], nbuf.at[1], load_sem.at[4]),
        pltpu.make_async_copy(cache_k.at[0], cbuf.at[0], load_sem.at[5]),
        pltpu.make_async_copy(cache_v.at[0], cbuf.at[1], load_sem.at[6]),
        pltpu.make_async_copy(pre_q.at[0], qbuf, load_sem.at[7]),
    ]
    own_k = pltpu.make_async_copy(pre_k.at[0], kbuf.at[tp], own_sem.at[0])
    own_v = pltpu.make_async_copy(pre_v.at[0], vbuf.at[tp], own_sem.at[1])

    barrier = pltpu.get_barrier_semaphore()

    def greet_replicas(k, _):
        s, g = shifted(k)
        pl.semaphore_signal(barrier, inc=1, device_id=(s, g, tp), device_id_type=MESH)
        return 0

    def greet_siblings(k, _):
        pl.semaphore_signal(barrier, inc=1, device_id=(sec, grp, sibling(k)), device_id_type=MESH)
        return 0

    lax.fori_loop(1, REPS, greet_replicas, 0)
    lax.fori_loop(1, NTP, greet_siblings, 0)
    for copy in loads:
        copy.start()
    own_k.start()
    own_v.start()
    pl.semaphore_wait(barrier, REPS - 1 + NTP - 1)

    def vouch(k, _):
        pl.semaphore_signal(ready, inc=1, device_id=(sec, grp, sibling(k)), device_id_type=MESH)
        return 0

    lax.fori_loop(1, NTP, vouch, 0)

    def chip_at(j):
        return lax.rem(y + jnp.where(j == 0, 0, jnp.where(j == 1, 1, jnp.where(j == 2, 3, 2))), 4)

    def uses(holder, user):
        return jnp.logical_or(holder < 3, user >= 2)

    def kv_direct(j, kv):
        source = (pre_k, pre_v)[kv]
        buf = (kbuf, vbuf)[kv]
        peer = other if j == 0 else chip_at(j) * 2 + core
        return pltpu.make_async_remote_copy(
            src_ref=source.at[0],
            dst_ref=buf.at[tp],
            send_sem=kv_send.at[kv, j],
            recv_sem=kv_recv.at[kv, tp],
            device_id=(sec, grp, peer),
            device_id_type=MESH,
        )

    def kv_relayed(yy, kv):
        buf = (kbuf, vbuf)[kv]
        chunk = yy * 2 + core
        return pltpu.make_async_remote_copy(
            src_ref=buf.at[chunk],
            dst_ref=buf.at[chunk],
            send_sem=kv_relay.at[kv, yy],
            recv_sem=kv_recv.at[kv, chunk],
            device_id=(sec, grp, other),
            device_id_type=MESH,
        )

    def kv_arrival(chunk, kv):
        buf = (kbuf, vbuf)[kv]
        return pltpu.make_async_copy(buf.at[chunk], buf.at[chunk], kv_recv.at[kv, chunk])

    for j in (1, 2, 3, 0):
        @pl.when(uses(y, chip_at(j)))
        def _():
            kv_direct(j, 0).start()
            kv_direct(j, 1).start()

    pl.semaphore_wait(ready, NTP - 1)
    loads[0].wait()
    loads[1].wait()
    token = lax.broadcasted_iota(jnp.int32, (BLOCK, KVH * HD), 0)

    def pack(owner):
        for slot in range(CAP):
            block = table[0, owner * CAP + slot]
            live = table[1, owner * CAP + slot]
            keep = token < live
            for kv in range(2):
                rows = poolbuf[kv, block]
                rows = jnp.where(keep, rows, jnp.zeros_like(rows))
                for t in range(NTP):
                    sendbuf[owner * NTP + t, kv * CAP + slot] = rows[:, t * HD : (t + 1) * HD]

    def page_copy(s, g, t):
        return pltpu.make_async_remote_copy(
            src_ref=sendbuf.at[(s * 16 + g) * NTP + t],
            dst_ref=pages.at[me],
            send_sem=page_send,
            recv_sem=page_recv,
            device_id=(s, g, t),
            device_id_type=MESH,
        )

    def hand_off(k, _):
        s, g = shifted(k)
        pack(s * 16 + g)
        for i in range(NTP):
            page_copy(s, g, sibling(i)).start()
        return 0

    lax.fori_loop(1, REPS, hand_off, 0)
    pack(sec * 16 + grp)
    for i in range(1, NTP):
        page_copy(sec, grp, sibling(i)).start()
    pltpu.make_async_copy(sendbuf.at[me], pages.at[me], page_recv).start()

    for copy in loads[2:]:
        copy.wait()
    shape = (STEPS * G * 16, 16 * CACHE)
    row = lax.broadcasted_iota(jnp.int32, shape, 0)
    col = lax.broadcasted_iota(jnp.int32, shape, 1)
    same_row = lax.rem(row, 16) == col // CACHE
    slot_of = lax.rem(col, CACHE)
    shape = (STEPS * G * 16, STEPS * 16)
    row = lax.broadcasted_iota(jnp.int32, shape, 0)
    col = lax.broadcasted_iota(jnp.int32, shape, 1)
    fresh_ok = jnp.logical_and(lax.rem(row, 16) == lax.rem(col, 16), col // 16 <= row // (G * 16))
    over_d = (((1,), (1,)), ((), ()))

    def decode(i, _):
        rows = pl.ds(pl.multiple_of(i * 16, 16), 16)
        query = jnp.concatenate(
            [dqbuf[s, rows, h * HD : (h + 1) * HD] for s in range(STEPS) for h in range(G)], axis=0
        )
        res_k = cbuf[0, rows].reshape(16 * CACHE, HD)
        res_v = cbuf[1, rows].reshape(16 * CACHE, HD)
        fresh_k = jnp.concatenate([nbuf[0, s, rows] for s in range(STEPS)], axis=0)
        fresh_v = jnp.concatenate([nbuf[1, s, rows] for s in range(STEPS)], axis=0)
        s1 = lax.dot_general(query, res_k, over_d, preferred_element_type=jnp.float32)
        s2 = lax.dot_general(query, fresh_k, over_d, preferred_element_type=jnp.float32)
        ok = jnp.logical_and(same_row, slot_of < lens[i])
        s1 = jnp.where(ok, s1 * LOG2E_SCALE, MASKED)
        s2 = jnp.where(fresh_ok, s2 * LOG2E_SCALE, MASKED)
        peak = jnp.maximum(jnp.max(s1, axis=1, keepdims=True), jnp.max(s2, axis=1, keepdims=True))
        p1 = jnp.exp2(s1 - peak)
        p2 = jnp.exp2(s2 - peak)
        mass = jnp.sum(p1, axis=1, keepdims=True) + jnp.sum(p2, axis=1, keepdims=True)
        out = jnp.dot(p1.astype(jnp.bfloat16), res_v, preferred_element_type=jnp.float32)
        out = out + jnp.dot(p2.astype(jnp.bfloat16), fresh_v, preferred_element_type=jnp.float32)
        out = (out / mass).astype(jnp.bfloat16)
        for s in range(STEPS):
            for h in range(G):
                part = (s * G + h) * 16
                dobuf[s, rows, h * HD : (h + 1) * HD] = out[part : part + 16]
        return 0

    lax.fori_loop(0, ROWS // 16, decode, 0)
    dec_store = pltpu.make_async_copy(dobuf, dec_out.at[0], store_sem.at[0])
    dec_store.start()

    top[...] = jnp.full_like(top, MASKED)
    total[...] = jnp.zeros_like(total)
    accum[...] = jnp.zeros_like(accum)
    shape = (ROW_TILE, CHIP_KEYS)
    ahead = lax.broadcasted_iota(jnp.int32, shape, 1) - lax.rem(
        lax.broadcasted_iota(jnp.int32, shape, 0), SPAN_DEV
    )
    ones = jnp.ones((CHIP_KEYS, HD), jnp.bfloat16)

    def attend(yy):
        reach = PRIOR + SPAN_DEV * tp - CHIP_KEYS * yy
        allowed = ahead <= reach

        def head(g, _):
            lanes = pl.ds(pl.multiple_of(g * HD, HD), HD)
            keys = kbuf[pl.ds(yy * 2, 2), :, lanes].reshape(CHIP_KEYS, HD)
            values = vbuf[pl.ds(yy * 2, 2), :, lanes].reshape(CHIP_KEYS, HD)
            values = jnp.concatenate([values, ones], axis=1)
            for part in range(G * SPAN_DEV // ROW_TILE):
                where = pl.ds(part * ROW_TILE, ROW_TILE)
                heads = ROW_TILE // SPAN_DEV
                query = jnp.concatenate(
                    [
                        qbuf[:, pl.ds(pl.multiple_of((g * G + part * heads + h) * HD, HD), HD)]
                        for h in range(heads)
                    ],
                    axis=0,
                )
                s = lax.dot_general(query, keys, over_d, preferred_element_type=jnp.float32)
                s = jnp.where(allowed, s * LOG2E_SCALE, MASKED)
                old = top[g, where]
                new = jnp.maximum(old, jnp.max(s, axis=1, keepdims=True))
                top[g, where] = new
                weights = jnp.exp2(s - jnp.concatenate([new] * (CHIP_KEYS // HD), axis=1))
                mix = jnp.dot(weights.astype(jnp.bfloat16), values, preferred_element_type=jnp.float32)
                fade = jnp.exp2(old - new)
                accum[g, where] = accum[g, where] * fade + mix[:, :HD]
                total[g, where] = total[g, where] * fade + mix[:, HD:]
            return 0

        lax.fori_loop(0, KVH, head, 0)

    own_k.wait()
    own_v.wait()

    def step(j, _):
        here = chip_at(j)
        later = chip_at(j + 1)

        @pl.when(jnp.logical_and(j < 3, uses(later, y)))
        def _():
            for kv in range(2):
                kv_arrival(later * 2 + core, kv).wait()
                kv_relayed(later, kv).start()

        @pl.when(uses(here, y))
        def _():
            for kv in range(2):
                kv_arrival(here * 2 + 1 - core, kv).wait()
            attend(here)

        return 0

    lax.fori_loop(0, 4, step, 0)

    def finish(g, _):
        for h in range(G):
            where = pl.ds(h * SPAN_DEV, SPAN_DEV)
            lanes = pl.ds(pl.multiple_of((g * G + h) * HD, HD), HD)
            obuf[:, lanes] = (accum[g, where] / total[g, where]).astype(jnp.bfloat16)
        return 0

    lax.fori_loop(0, KVH, finish, 0)
    pre_store = pltpu.make_async_copy(obuf, pre_out.at[0], store_sem.at[1])
    pre_store.start()

    for j in range(4):
        @pl.when(uses(y, chip_at(j)))
        def _():
            kv_direct(j, 0).wait_send()
            kv_direct(j, 1).wait_send()

    for j in range(1, 4):
        @pl.when(uses(chip_at(j), y))
        def _():
            kv_relayed(chip_at(j), 0).wait_send()
            kv_relayed(chip_at(j), 1).wait_send()

    dec_store.wait()
    pre_store.wait()
    some = pl.ds(0, UNITS - 1)
    pltpu.make_async_copy(sendbuf.at[some], sendbuf.at[some], page_send).wait()
    pltpu.make_async_copy(pages, pages, page_recv).wait()


def block_table(owners, counts):
    blocks = jnp.arange(owners.shape[0], dtype=jnp.int32)
    earlier = (owners[None, :] == owners[:, None]) & (blocks[None, :] < blocks[:, None])
    slot = jnp.sum(earlier.astype(jnp.int32), axis=1)
    place = owners * CAP + slot
    chosen = place[None, :] == jnp.arange(REPS * CAP, dtype=jnp.int32)[:, None]
    pair = jnp.stack([blocks, counts])
    return jnp.sum(jnp.where(chosen[None], pair[:, None, :], 0), axis=2)


def body(
    pre_query,
    pre_keys,
    pre_values,
    dec_query,
    dec_new_keys,
    dec_new_values,
    cache_keys,
    cache_values,
    cache_lens,
    pool_keys,
    pool_values,
    block_owner,
    block_count,
):
    table = block_table(block_owner[0, 0, :, 0], block_count[0, 0])
    lens = jnp.repeat(cache_lens[0], CACHE).reshape(ROWS // 16, 1, 16 * CACHE)
    bf16, f32 = jnp.bfloat16, jnp.float32
    anywhere = pl.BlockSpec(memory_space=pl.ANY)
    pre_out, dec_out, pages = pl.pallas_call(
        kernel,
        out_shape=(
            jax.ShapeDtypeStruct((1, SPAN_DEV, H * HD), bf16),
            jax.ShapeDtypeStruct((1, STEPS, ROWS, G * HD), bf16),
            jax.ShapeDtypeStruct((UNITS, 2 * CAP, BLOCK, HD), bf16),
        ),
        in_specs=[pl.BlockSpec(memory_space=pltpu.SMEM), pl.BlockSpec(memory_space=pltpu.VMEM)] + [anywhere] * 10,
        out_specs=(anywhere, anywhere, anywhere),
        scratch_shapes=[
            pltpu.VMEM((SPAN_DEV, H * HD), bf16),
            pltpu.VMEM((NTP, KEY_DEV, KVH * HD), bf16),
            pltpu.VMEM((NTP, KEY_DEV, KVH * HD), bf16),
            pltpu.VMEM((2, 32, BLOCK, KVH * HD), bf16),
            pltpu.VMEM((UNITS, 2 * CAP, BLOCK, HD), bf16),
            pltpu.VMEM((KVH, G * SPAN_DEV, HD), f32),
            pltpu.VMEM((KVH, G * SPAN_DEV, HD), f32),
            pltpu.VMEM((KVH, G * SPAN_DEV, HD), f32),
            pltpu.VMEM((SPAN_DEV, H * HD), bf16),
            pltpu.VMEM((STEPS, ROWS, G * HD), bf16),
            pltpu.VMEM((2, STEPS, ROWS, HD), bf16),
            pltpu.VMEM((2, ROWS, CACHE, HD), bf16),
            pltpu.VMEM((STEPS, ROWS, G * HD), bf16),
            pltpu.SemaphoreType.REGULAR,
            pltpu.SemaphoreType.DMA((8,)),
            pltpu.SemaphoreType.DMA((2,)),
            pltpu.SemaphoreType.DMA((2, 4)),
            pltpu.SemaphoreType.DMA((2, 4)),
            pltpu.SemaphoreType.DMA((2, 8)),
            pltpu.SemaphoreType.DMA,
            pltpu.SemaphoreType.DMA,
            pltpu.SemaphoreType.DMA((2,)),
        ],
        compiler_params=pltpu.CompilerParams(
            collective_id=0, has_side_effects=True, vmem_limit_bytes=56 * 2**20
        ),
    )(
        table,
        lens,
        pre_query,
        pre_keys,
        pre_values,
        dec_query,
        dec_new_keys,
        dec_new_values,
        cache_keys,
        cache_values,
        pool_keys,
        pool_values,
    )
    pages = pages.reshape(1, REPS, NTP, 2, CAP, BLOCK, HD)
    return pre_out, dec_out, pages[:, :, :, 0], pages[:, :, :, 1]


def solution(mesh):
    return jax.shard_map(
        body,
        mesh=mesh,
        in_specs=(
            P(("sec", "grp"), "tp", None),
            P(("sec", "grp"), "tp", None),
            P(("sec", "grp"), "tp", None),
            P(("sec", "grp"), None, None, "tp"),
            P(("sec", "grp"), None, None, "tp"),
            P(("sec", "grp"), None, None, "tp"),
            P(("sec", "grp"), None, None, "tp"),
            P(("sec", "grp"), None, None, "tp"),
            P(("sec", "grp"), None),
            P(("sec", "grp"), "tp", None, None, None),
            P(("sec", "grp"), "tp", None, None, None),
            P(("sec", "grp"), "tp", None, None),
            P(("sec", "grp"), "tp", None),
        ),
        out_specs=(
            P(("sec", "grp"), "tp", None),
            P(("sec", "grp"), None, None, "tp"),
            P(("sec", "grp"), None, None, None, None, "tp"),
            P(("sec", "grp"), None, None, None, None, "tp"),
        ),
        check_vma=False,
    )
```

```python
import jax
import jax.numpy as jnp
from jax import lax
from jax.experimental import pallas as pl
from jax.experimental.pallas import tpu as pltpu
from jax.sharding import PartitionSpec as P

H = 64
KVH = 8
HD = 128
G = 8
CAP = 2
BLOCK = 16
REPS = 32
NTP = 8
SPAN_DEV = 128
KEY_DEV = 256
CHIP_KEYS = 2 * KEY_DEV
PRIOR = 1024
ROWS = 64
STEPS = 2
CACHE = 16
UNITS = REPS * NTP
ROW_TILE = 256
LOG2E_SCALE = 1.4426950408889634 * HD**-0.5
MASKED = -1e30
MESH = pl.DeviceIdType.MESH


def position():
    sec, grp, tp = lax.axis_index("sec"), lax.axis_index("grp"), lax.axis_index("tp")
    return grp // 4, tp // 2, sec * 4 + lax.rem(grp, 4), lax.rem(tp, 2)


def replica_at(x, z):
    return z // 4, x * 4 + lax.rem(z, 4)


def kernel(
    owners,
    counts,
    lens,
    pre_q,
    pre_k,
    pre_v,
    dec_q,
    new_k,
    new_v,
    cache_k,
    cache_v,
    pool_k,
    pool_v,
    pre_out,
    dec_out,
    pages_k,
    pages_v,
    qbuf,
    kbuf,
    vbuf,
    poolbuf,
    sendbuf,
    top,
    total,
    accum,
    obuf,
    dqbuf,
    nbuf,
    cbuf,
    dobuf,
    lenbuf,
    codebuf,
    table,
    ready,
    load_sem,
    table_sem,
    own_sem,
    kv_send,
    kv_onward,
    kv_relay,
    kv_recv,
    page_send,
    page_recv,
    store_sem,
):
    x, y, z, core = position()
    sec, grp, tp = lax.axis_index("sec"), lax.axis_index("grp"), lax.axis_index("tp")
    me = (sec * 16 + grp) * NTP + tp
    other = y * 2 + 1 - core

    def shifted(k):
        return replica_at(lax.rem(x + k // 8, 4), lax.rem(z + lax.rem(k, 8), 8))

    def sibling(k):
        return lax.rem(tp + k, NTP)

    pages = (pages_k, pages_v)

    loads = [
        pltpu.make_async_copy(pool_k.at[0, 0], poolbuf.at[0], load_sem.at[0]),
        pltpu.make_async_copy(pool_v.at[0, 0], poolbuf.at[1], load_sem.at[1]),
        pltpu.make_async_copy(dec_q.at[0], dqbuf, load_sem.at[2]),
        pltpu.make_async_copy(new_k.at[0], nbuf.at[0], load_sem.at[3]),
        pltpu.make_async_copy(new_v.at[0], nbuf.at[1], load_sem.at[4]),
        pltpu.make_async_copy(cache_k.at[0], cbuf.at[0], load_sem.at[5]),
        pltpu.make_async_copy(cache_v.at[0], cbuf.at[1], load_sem.at[6]),
        pltpu.make_async_copy(pre_q.at[0], qbuf, load_sem.at[7]),
    ]
    own_k = pltpu.make_async_copy(pre_k.at[0], kbuf.at[tp], own_sem.at[0])
    own_v = pltpu.make_async_copy(pre_v.at[0], vbuf.at[tp], own_sem.at[1])

    barrier = pltpu.get_barrier_semaphore()

    def greet_replicas(k, _):
        s, g = shifted(k)
        pl.semaphore_signal(barrier, inc=1, device_id=(s, g, tp), device_id_type=MESH)
        return 0

    def greet_siblings(k, _):
        pl.semaphore_signal(barrier, inc=1, device_id=(sec, grp, sibling(k)), device_id_type=MESH)
        return 0

    lax.fori_loop(1, REPS, greet_replicas, 0)
    lax.fori_loop(1, NTP, greet_siblings, 0)
    for copy in loads:
        copy.start()
    own_k.start()
    own_v.start()

    pool_len = owners.shape[2]
    first = lax.broadcasted_iota(jnp.int32, (pool_len, pool_len), 0)
    second = lax.broadcasted_iota(jnp.int32, (pool_len, pool_len), 1)
    same = first == second
    owner_col = owners[0, 0]
    owner_row = jnp.sum(jnp.where(same, owner_col, 0), axis=0, keepdims=True)
    count_col = jnp.sum(jnp.where(same, counts[0], 0), axis=1, keepdims=True)
    earlier = jnp.logical_and(owner_row == owner_col, second < first)
    slot_col = jnp.sum(jnp.where(earlier, 1, 0), axis=1, keepdims=True)
    chosen = owner_col * CAP + slot_col == lax.broadcasted_iota(jnp.int32, (pool_len, 128), 1)
    block_col = lax.broadcasted_iota(jnp.int32, (pool_len, 128), 0)
    codebuf[0:1] = jnp.sum(jnp.where(chosen, block_col, 0), axis=0, keepdims=True)
    codebuf[1:2] = jnp.sum(jnp.where(chosen, count_col, 0), axis=0, keepdims=True)
    to_scalars = pltpu.make_async_copy(codebuf, table, table_sem)
    to_scalars.start()
    first = lax.broadcasted_iota(jnp.int32, (ROWS, ROWS), 0)
    second = lax.broadcasted_iota(jnp.int32, (ROWS, ROWS), 1)
    len_col = jnp.sum(jnp.where(first == second, lens[...], 0), axis=1, keepdims=True)
    lenbuf[...] = jnp.broadcast_to(len_col, lenbuf.shape)
    to_scalars.wait()

    loads[0].wait()
    loads[1].wait()
    token = lax.broadcasted_iota(jnp.int32, (BLOCK, KVH * HD), 0)

    def pack(owner, _):
        for slot in range(CAP):
            block = table[0, owner * CAP + slot]
            live = table[1, owner * CAP + slot]
            keep = token < live
            for kv in range(2):
                rows = poolbuf[kv, block]
                rows = jnp.where(keep, rows, jnp.zeros_like(rows))
                for t in range(NTP):
                    sendbuf[kv, owner * NTP + t, slot] = rows[:, t * HD : (t + 1) * HD]
        return 0

    lax.fori_loop(0, REPS, pack, 0)
    pl.semaphore_wait(barrier, REPS - 1 + NTP - 1)

    def vouch(k, _):
        pl.semaphore_signal(ready, inc=1, device_id=(sec, grp, sibling(k)), device_id_type=MESH)
        return 0

    lax.fori_loop(1, NTP, vouch, 0)

    def chip_at(j):
        return lax.rem(y + jnp.where(j == 0, 0, jnp.where(j == 1, 1, jnp.where(j == 2, 3, 2))), 4)

    def uses(holder, user):
        return jnp.logical_or(holder < 3, user >= 2)

    def kv_direct(j, kv):
        source = (pre_k, pre_v)[kv]
        buf = (kbuf, vbuf)[kv]
        peer = other if j == 0 else chip_at(j) * 2 + core
        return pltpu.make_async_remote_copy(
            src_ref=source.at[0],
            dst_ref=buf.at[tp],
            send_sem=kv_send.at[kv, j],
            recv_sem=kv_recv.at[kv, tp],
            device_id=(sec, grp, peer),
            device_id_type=MESH,
        )

    def kv_forward(kv):
        buf = (kbuf, vbuf)[kv]
        source, target = (chip_at(2), chip_at(1)) if kv == 0 else (chip_at(1), chip_at(2))
        chunk = source * 2 + core
        return pltpu.make_async_remote_copy(
            src_ref=buf.at[chunk],
            dst_ref=buf.at[chunk],
            send_sem=kv_onward.at[kv],
            recv_sem=kv_recv.at[kv, chunk],
            device_id=(sec, grp, target * 2 + core),
            device_id_type=MESH,
        )

    def forwards(kv):
        source, target = (chip_at(2), chip_at(1)) if kv == 0 else (chip_at(1), chip_at(2))
        return jnp.logical_and(uses(source, y), uses(source, target))

    def kv_relayed(yy, kv):
        buf = (kbuf, vbuf)[kv]
        chunk = yy * 2 + core
        return pltpu.make_async_remote_copy(
            src_ref=buf.at[chunk],
            dst_ref=buf.at[chunk],
            send_sem=kv_relay.at[kv, yy],
            recv_sem=kv_recv.at[kv, chunk],
            device_id=(sec, grp, other),
            device_id_type=MESH,
        )

    def kv_arrival(chunk, kv):
        buf = (kbuf, vbuf)[kv]
        return pltpu.make_async_copy(buf.at[chunk], buf.at[chunk], kv_recv.at[kv, chunk])

    for j in (1, 2, 0):
        @pl.when(uses(y, chip_at(j)))
        def _():
            kv_direct(j, 0).start()
            kv_direct(j, 1).start()

    pl.semaphore_wait(ready, NTP - 1)

    def page_copy(kv, s, g, t):
        return pltpu.make_async_remote_copy(
            src_ref=sendbuf.at[kv, (s * 16 + g) * NTP + t],
            dst_ref=pages[kv].at[me],
            send_sem=page_send.at[kv],
            recv_sem=page_recv.at[kv],
            device_id=(s, g, t),
            device_id_type=MESH,
        )

    def hand_off(k, _):
        s, g = replica_at(lax.rem(x + lax.rem(k // 8, 4), 4), lax.rem(z + lax.rem(k, 8), 8))
        t = lax.rem(y + k // 64, 4) * 2 + lax.rem(core + lax.rem(k // 32, 2), 2)
        page_copy(0, s, g, t).start()
        page_copy(1, s, g, t).start()
        return 0

    quarter = UNITS // 4
    lax.fori_loop(1, quarter, hand_off, 0)
    for kv in range(2):
        pltpu.make_async_copy(sendbuf.at[kv, me], pages[kv].at[me], page_recv.at[kv]).start()

    for copy in loads[2:]:
        copy.wait()
    shape = (STEPS * G * 16, 16 * CACHE)
    row = lax.broadcasted_iota(jnp.int32, shape, 0)
    col = lax.broadcasted_iota(jnp.int32, shape, 1)
    same_row = lax.rem(row, 16) == col // CACHE
    slot_of = lax.rem(col, CACHE)
    shape = (STEPS * G * 16, STEPS * 16)
    row = lax.broadcasted_iota(jnp.int32, shape, 0)
    col = lax.broadcasted_iota(jnp.int32, shape, 1)
    fresh_ok = jnp.logical_and(lax.rem(row, 16) == lax.rem(col, 16), col // 16 <= row // (G * 16))
    over_d = (((1,), (1,)), ((), ()))

    def decode(i, _):
        rows = pl.ds(pl.multiple_of(i * 16, 16), 16)
        query = jnp.concatenate(
            [dqbuf[s, rows, h * HD : (h + 1) * HD] for s in range(STEPS) for h in range(G)], axis=0
        )
        res_k = cbuf[0, rows].reshape(16 * CACHE, HD)
        res_v = cbuf[1, rows].reshape(16 * CACHE, HD)
        fresh_k = jnp.concatenate([nbuf[0, s, rows] for s in range(STEPS)], axis=0)
        fresh_v = jnp.concatenate([nbuf[1, s, rows] for s in range(STEPS)], axis=0)
        s1 = lax.dot_general(query, res_k, over_d, preferred_element_type=jnp.float32)
        s2 = lax.dot_general(query, fresh_k, over_d, preferred_element_type=jnp.float32)
        live = jnp.concatenate([lenbuf[rows]] * (STEPS * G), axis=0)
        ok = jnp.logical_and(same_row, slot_of < jnp.concatenate([live] * (16 * CACHE // HD), axis=1))
        s1 = jnp.where(ok, s1 * LOG2E_SCALE, MASKED)
        s2 = jnp.where(fresh_ok, s2 * LOG2E_SCALE, MASKED)
        peak = jnp.maximum(jnp.max(s1, axis=1, keepdims=True), jnp.max(s2, axis=1, keepdims=True))
        p1 = jnp.exp2(s1 - peak)
        p2 = jnp.exp2(s2 - peak)
        mass = jnp.sum(p1, axis=1, keepdims=True) + jnp.sum(p2, axis=1, keepdims=True)
        out = jnp.dot(p1.astype(jnp.bfloat16), res_v, preferred_element_type=jnp.float32)
        out = out + jnp.dot(p2.astype(jnp.bfloat16), fresh_v, preferred_element_type=jnp.float32)
        out = (out / mass).astype(jnp.bfloat16)
        for s in range(STEPS):
            for h in range(G):
                part = (s * G + h) * 16
                dobuf[s, rows, h * HD : (h + 1) * HD] = out[part : part + 16]
        return 0

    lax.fori_loop(0, ROWS // 16, decode, 0)
    dec_store = pltpu.make_async_copy(dobuf, dec_out.at[0], store_sem.at[0])
    dec_store.start()

    top[...] = jnp.full_like(top, MASKED)
    total[...] = jnp.zeros_like(total)
    accum[...] = jnp.zeros_like(accum)
    shape = (ROW_TILE, CHIP_KEYS)
    ahead = lax.broadcasted_iota(jnp.int32, shape, 1) - lax.rem(
        lax.broadcasted_iota(jnp.int32, shape, 0), SPAN_DEV
    )
    ones = jnp.ones((CHIP_KEYS, HD), jnp.bfloat16)

    def attend(yy, reach, masked):
        allowed = ahead <= reach

        def head(g, _):
            lanes = pl.ds(pl.multiple_of(g * HD, HD), HD)
            keys = kbuf[pl.ds(yy * 2, 2), :, lanes].reshape(CHIP_KEYS, HD)
            values = vbuf[pl.ds(yy * 2, 2), :, lanes].reshape(CHIP_KEYS, HD)
            values = jnp.concatenate([values, ones], axis=1)
            parts = G * SPAN_DEV // ROW_TILE
            heads = ROW_TILE // SPAN_DEV

            def scores(part):
                query = jnp.concatenate(
                    [
                        qbuf[:, pl.ds(pl.multiple_of((g * G + part * heads + h) * HD, HD), HD)]
                        for h in range(heads)
                    ],
                    axis=0,
                )
                return lax.dot_general(query, keys, over_d, preferred_element_type=jnp.float32)

            s = scores(0)
            for part in range(parts):
                following = scores(part + 1) if part + 1 < parts else None
                where = pl.ds(part * ROW_TILE, ROW_TILE)
                s = s * LOG2E_SCALE
                if masked:
                    s = jnp.where(allowed, s, MASKED)
                old = top[g, where]
                new = jnp.maximum(old, jnp.max(s, axis=1, keepdims=True))
                weights = jnp.exp2(s - jnp.concatenate([new] * (CHIP_KEYS // HD), axis=1))
                fade = jnp.exp2(old - new)
                mix = jnp.dot(weights.astype(jnp.bfloat16), values, preferred_element_type=jnp.float32)
                top[g, where] = new
                accum[g, where] = accum[g, where] * fade + mix[:, :HD]
                total[g, where] = total[g, where] * fade + mix[:, HD:]
                s = following
            return 0

        lax.fori_loop(0, KVH, head, 0)

    own_k.wait()
    own_v.wait()

    def relay(j, kv):
        kv_arrival(chip_at(j) * 2 + core, kv).wait()
        kv_relayed(chip_at(j), kv).start()

    def step(j, _):
        here = chip_at(j)

        @pl.when(j == 1)
        def _():
            lax.fori_loop(quarter, 2 * quarter, hand_off, 0)

            @pl.when(uses(chip_at(2), y))
            def _():
                relay(2, 0)

            @pl.when(forwards(0))
            def _():
                kv_forward(0).start()

            @pl.when(uses(chip_at(1), y))
            def _():
                relay(1, 1)

            @pl.when(forwards(1))
            def _():
                kv_forward(1).start()

            @pl.when(uses(chip_at(1), y))
            def _():
                relay(1, 0)

            @pl.when(uses(chip_at(2), y))
            def _():
                relay(2, 1)

        @pl.when(j == 2)
        def _():
            lax.fori_loop(2 * quarter, 4 * quarter, hand_off, 0)

        @pl.when(jnp.logical_and(j == 2, uses(chip_at(3), y)))
        def _():
            relay(3, 0)
            relay(3, 1)

        @pl.when(uses(here, y))
        def _():
            for kv in range(2):
                kv_arrival(here * 2 + 1 - core, kv).wait()
            reach = PRIOR + SPAN_DEV * tp - CHIP_KEYS * here

            @pl.when(reach < CHIP_KEYS - 1)
            def _():
                attend(here, reach, True)

            @pl.when(reach >= CHIP_KEYS - 1)
            def _():
                attend(here, reach, False)

        return 0

    lax.fori_loop(0, 4, step, 0)

    def finish(g, _):
        for h in range(G):
            where = pl.ds(h * SPAN_DEV, SPAN_DEV)
            lanes = pl.ds(pl.multiple_of((g * G + h) * HD, HD), HD)
            obuf[:, lanes] = (accum[g, where] / total[g, where]).astype(jnp.bfloat16)
        return 0

    lax.fori_loop(0, KVH, finish, 0)
    pre_store = pltpu.make_async_copy(obuf, pre_out.at[0], store_sem.at[1])
    pre_store.start()

    for j in range(3):
        @pl.when(uses(y, chip_at(j)))
        def _():
            kv_direct(j, 0).wait_send()
            kv_direct(j, 1).wait_send()

    for kv in range(2):
        @pl.when(forwards(kv))
        def _():
            kv_forward(kv).wait_send()

    for j in range(1, 4):
        @pl.when(uses(chip_at(j), y))
        def _():
            kv_relayed(chip_at(j), 0).wait_send()
            kv_relayed(chip_at(j), 1).wait_send()

    dec_store.wait()
    pre_store.wait()
    some = pl.ds(0, UNITS - 1)
    for kv in range(2):
        pltpu.make_async_copy(sendbuf.at[kv, some], sendbuf.at[kv, some], page_send.at[kv]).wait()
        pltpu.make_async_copy(pages[kv], pages[kv], page_recv.at[kv]).wait()


def body(
    pre_query,
    pre_keys,
    pre_values,
    dec_query,
    dec_new_keys,
    dec_new_values,
    cache_keys,
    cache_values,
    cache_lens,
    pool_keys,
    pool_values,
    block_owner,
    block_count,
):
    bf16, f32 = jnp.bfloat16, jnp.float32
    anywhere = pl.BlockSpec(memory_space=pl.ANY)
    pre_out, dec_out, pages_keys, pages_values = pl.pallas_call(
        kernel,
        out_shape=(
            jax.ShapeDtypeStruct((1, SPAN_DEV, H * HD), bf16),
            jax.ShapeDtypeStruct((1, STEPS, ROWS, G * HD), bf16),
            jax.ShapeDtypeStruct((UNITS, CAP, BLOCK, HD), bf16),
            jax.ShapeDtypeStruct((UNITS, CAP, BLOCK, HD), bf16),
        ),
        in_specs=[pl.BlockSpec(memory_space=pltpu.VMEM)] * 3 + [anywhere] * 10,
        out_specs=(anywhere,) * 4,
        scratch_shapes=[
            pltpu.VMEM((SPAN_DEV, H * HD), bf16),
            pltpu.VMEM((NTP, KEY_DEV, KVH * HD), bf16),
            pltpu.VMEM((NTP, KEY_DEV, KVH * HD), bf16),
            pltpu.VMEM((2, 32, BLOCK, KVH * HD), bf16),
            pltpu.VMEM((2, UNITS, CAP, BLOCK, HD), bf16),
            pltpu.VMEM((KVH, G * SPAN_DEV, HD), f32),
            pltpu.VMEM((KVH, G * SPAN_DEV, HD), f32),
            pltpu.VMEM((KVH, G * SPAN_DEV, HD), f32),
            pltpu.VMEM((SPAN_DEV, H * HD), bf16),
            pltpu.VMEM((STEPS, ROWS, G * HD), bf16),
            pltpu.VMEM((2, STEPS, ROWS, HD), bf16),
            pltpu.VMEM((2, ROWS, CACHE, HD), bf16),
            pltpu.VMEM((STEPS, ROWS, G * HD), bf16),
            pltpu.VMEM((ROWS, HD), jnp.int32),
            pltpu.VMEM((2, HD), jnp.int32),
            pltpu.SMEM((2, HD), jnp.int32),
            pltpu.SemaphoreType.REGULAR,
            pltpu.SemaphoreType.DMA((8,)),
            pltpu.SemaphoreType.DMA,
            pltpu.SemaphoreType.DMA((2,)),
            pltpu.SemaphoreType.DMA((2, 3)),
            pltpu.SemaphoreType.DMA((2,)),
            pltpu.SemaphoreType.DMA((2, 4)),
            pltpu.SemaphoreType.DMA((2, 8)),
            pltpu.SemaphoreType.DMA((2,)),
            pltpu.SemaphoreType.DMA((2,)),
            pltpu.SemaphoreType.DMA((2,)),
        ],
        compiler_params=pltpu.CompilerParams(
            collective_id=0, has_side_effects=True, vmem_limit_bytes=56 * 2**20
        ),
    )(
        block_owner,
        block_count,
        cache_lens,
        pre_query,
        pre_keys,
        pre_values,
        dec_query,
        dec_new_keys,
        dec_new_values,
        cache_keys,
        cache_values,
        pool_keys,
        pool_values,
    )
    shape = (1, REPS, NTP, CAP, BLOCK, HD)
    return pre_out, dec_out, pages_keys.reshape(shape), pages_values.reshape(shape)


def solution(mesh):
    return jax.shard_map(
        body,
        mesh=mesh,
        in_specs=(
            P(("sec", "grp"), "tp", None),
            P(("sec", "grp"), "tp", None),
            P(("sec", "grp"), "tp", None),
            P(("sec", "grp"), None, None, "tp"),
            P(("sec", "grp"), None, None, "tp"),
            P(("sec", "grp"), None, None, "tp"),
            P(("sec", "grp"), None, None, "tp"),
            P(("sec", "grp"), None, None, "tp"),
            P(("sec", "grp"), None),
            P(("sec", "grp"), "tp", None, None, None),
            P(("sec", "grp"), "tp", None, None, None),
            P(("sec", "grp"), "tp", None, None),
            P(("sec", "grp"), "tp", None),
        ),
        out_specs=(
            P(("sec", "grp"), "tp", None),
            P(("sec", "grp"), None, None, "tp"),
            P(("sec", "grp"), None, None, None, None, "tp"),
            P(("sec", "grp"), None, None, None, None, "tp"),
        ),
        check_vma=False,
    )
```

```python
import jax
import jax.numpy as jnp
from jax import lax
from jax.experimental import pallas as pl
from jax.experimental.pallas import tpu as pltpu
from jax.sharding import PartitionSpec as P

H = 64
KVH = 8
HD = 128
G = 8
CAP = 2
BLOCK = 16
REPS = 32
NTP = 8
SPAN_DEV = 128
KEY_DEV = 256
CHIP_KEYS = 2 * KEY_DEV
PRIOR = 1024
ROWS = 64
STEPS = 2
CACHE = 16
UNITS = REPS * NTP
ROW_TILE = 256
LOG2E_SCALE = 1.4426950408889634 * HD**-0.5
MASKED = -1e30
MESH = pl.DeviceIdType.MESH


def position():
    sec, grp, tp = lax.axis_index("sec"), lax.axis_index("grp"), lax.axis_index("tp")
    return grp // 4, tp // 2, sec * 4 + lax.rem(grp, 4), lax.rem(tp, 2)


def replica_at(x, z):
    return z // 4, x * 4 + lax.rem(z, 4)


def kernel(
    owners,
    counts,
    lens,
    pre_q,
    pre_k,
    pre_v,
    dec_q,
    new_k,
    new_v,
    cache_k,
    cache_v,
    pool_k,
    pool_v,
    pre_out,
    dec_out,
    pages_k,
    pages_v,
    qbuf,
    kbuf,
    vbuf,
    poolbuf,
    sendbuf,
    top,
    total,
    accum,
    dqbuf,
    nbuf,
    cbuf,
    lenbuf,
    codebuf,
    table,
    ready,
    load_sem,
    table_sem,
    own_sem,
    kv_send,
    kv_onward,
    kv_relay,
    kv_recv,
    page_send,
    page_recv,
):
    x, y, z, core = position()
    sec, grp, tp = lax.axis_index("sec"), lax.axis_index("grp"), lax.axis_index("tp")
    me = (sec * 16 + grp) * NTP + tp
    other = y * 2 + 1 - core

    def shifted(k):
        return replica_at(lax.rem(x + k // 8, 4), lax.rem(z + lax.rem(k, 8), 8))

    def sibling(k):
        return lax.rem(tp + k, NTP)

    pages = (pages_k, pages_v)

    loads = [
        pltpu.make_async_copy(pool_k.at[0, 0], poolbuf.at[0], load_sem.at[0]),
        pltpu.make_async_copy(pool_v.at[0, 0], poolbuf.at[1], load_sem.at[1]),
        pltpu.make_async_copy(dec_q.at[0], dqbuf, load_sem.at[2]),
        pltpu.make_async_copy(new_k.at[0], nbuf.at[0], load_sem.at[3]),
        pltpu.make_async_copy(new_v.at[0], nbuf.at[1], load_sem.at[4]),
        pltpu.make_async_copy(cache_k.at[0], cbuf.at[0], load_sem.at[5]),
        pltpu.make_async_copy(cache_v.at[0], cbuf.at[1], load_sem.at[6]),
        pltpu.make_async_copy(pre_q.at[0], qbuf, load_sem.at[7]),
    ]
    own_k = pltpu.make_async_copy(pre_k.at[0], kbuf.at[tp], own_sem.at[0])
    own_v = pltpu.make_async_copy(pre_v.at[0], vbuf.at[tp], own_sem.at[1])

    for copy in loads:
        copy.start()
    own_k.start()
    own_v.start()

    barrier = pltpu.get_barrier_semaphore()

    def greet_replicas(k, _):
        s, g = shifted(k)
        pl.semaphore_signal(barrier, inc=1, device_id=(s, g, tp), device_id_type=MESH)
        return 0

    def greet_siblings(k, _):
        pl.semaphore_signal(barrier, inc=1, device_id=(sec, grp, sibling(k)), device_id_type=MESH)
        return 0

    lax.fori_loop(1, REPS, greet_replicas, 0)
    lax.fori_loop(1, NTP, greet_siblings, 0)

    pool_len = owners.shape[1]
    first = lax.broadcasted_iota(jnp.int32, (pool_len, pool_len), 0)
    second = lax.broadcasted_iota(jnp.int32, (pool_len, pool_len), 1)
    same = first == second
    owner_row = owners[...]
    owner_col = jnp.sum(jnp.where(same, owner_row, 0), axis=1, keepdims=True)
    count_col = jnp.sum(jnp.where(same, counts[...], 0), axis=1, keepdims=True)
    earlier = jnp.logical_and(owner_row == owner_col, second < first)
    slot_col = jnp.sum(jnp.where(earlier, 1, 0), axis=1, keepdims=True)
    chosen = owner_col * CAP + slot_col == lax.broadcasted_iota(jnp.int32, (pool_len, 128), 1)
    block_col = lax.broadcasted_iota(jnp.int32, (pool_len, 128), 0)
    codebuf[0:1] = jnp.sum(jnp.where(chosen, block_col, 0), axis=0, keepdims=True)
    codebuf[1:2] = jnp.sum(jnp.where(chosen, count_col, 0), axis=0, keepdims=True)
    to_scalars = pltpu.make_async_copy(codebuf, table, table_sem)
    to_scalars.start()
    first = lax.broadcasted_iota(jnp.int32, (ROWS, ROWS), 0)
    second = lax.broadcasted_iota(jnp.int32, (ROWS, ROWS), 1)
    len_col = jnp.sum(jnp.where(first == second, lens[...], 0), axis=1, keepdims=True)
    lenbuf[...] = jnp.broadcast_to(len_col, lenbuf.shape)
    to_scalars.wait()

    loads[0].wait()
    loads[1].wait()
    token = lax.broadcasted_iota(jnp.int32, (BLOCK, HD), 0)
    blank = jnp.zeros((BLOCK, HD), jnp.bfloat16)

    def pack(owner, _):
        for slot in range(CAP):
            block = table[0, owner * CAP + slot]
            live = table[1, owner * CAP + slot]
            keep = token < live
            for kv in range(2):
                rows = poolbuf[kv, block]
                for t in range(NTP):
                    part = rows[:, t * HD : (t + 1) * HD]
                    sendbuf[kv, owner * NTP + t, slot] = jnp.where(keep, part, blank)
        return 0

    lax.fori_loop(0, REPS, pack, 0)
    pl.semaphore_wait(barrier, REPS - 1 + NTP - 1)

    def vouch(k, _):
        pl.semaphore_signal(ready, inc=1, device_id=(sec, grp, sibling(k)), device_id_type=MESH)
        return 0

    lax.fori_loop(1, NTP, vouch, 0)

    def chip_at(j):
        return lax.rem(y + jnp.where(j == 0, 0, jnp.where(j == 1, 1, jnp.where(j == 2, 3, 2))), 4)

    def uses(holder, user):
        return jnp.logical_or(holder < 3, user >= 2)

    def kv_direct(j, kv):
        source = (pre_k, pre_v)[kv]
        buf = (kbuf, vbuf)[kv]
        peer = other if j == 0 else chip_at(j) * 2 + core
        return pltpu.make_async_remote_copy(
            src_ref=source.at[0],
            dst_ref=buf.at[tp],
            send_sem=kv_send.at[kv, j],
            recv_sem=kv_recv.at[kv, tp],
            device_id=(sec, grp, peer),
            device_id_type=MESH,
        )

    def kv_forward(kv):
        buf = (kbuf, vbuf)[kv]
        source, target = (chip_at(2), chip_at(1)) if kv == 0 else (chip_at(1), chip_at(2))
        chunk = source * 2 + core
        return pltpu.make_async_remote_copy(
            src_ref=buf.at[chunk],
            dst_ref=buf.at[chunk],
            send_sem=kv_onward.at[kv],
            recv_sem=kv_recv.at[kv, chunk],
            device_id=(sec, grp, target * 2 + core),
            device_id_type=MESH,
        )

    def forwards(kv):
        source, target = (chip_at(2), chip_at(1)) if kv == 0 else (chip_at(1), chip_at(2))
        return jnp.logical_and(uses(source, y), uses(source, target))

    def kv_relayed(yy, kv):
        buf = (kbuf, vbuf)[kv]
        chunk = yy * 2 + core
        return pltpu.make_async_remote_copy(
            src_ref=buf.at[chunk],
            dst_ref=buf.at[chunk],
            send_sem=kv_relay.at[kv, yy],
            recv_sem=kv_recv.at[kv, chunk],
            device_id=(sec, grp, other),
            device_id_type=MESH,
        )

    def kv_arrival(chunk, kv):
        buf = (kbuf, vbuf)[kv]
        return pltpu.make_async_copy(buf.at[chunk], buf.at[chunk], kv_recv.at[kv, chunk])

    for j in (1, 2, 0):
        @pl.when(uses(y, chip_at(j)))
        def _():
            kv_direct(j, 0).start()
            kv_direct(j, 1).start()


    def page_copy(kv, s, g, t):
        return pltpu.make_async_remote_copy(
            src_ref=sendbuf.at[kv, (s * 16 + g) * NTP + t],
            dst_ref=pages[kv].at[me],
            send_sem=page_send.at[kv],
            recv_sem=page_recv.at[kv],
            device_id=(s, g, t),
            device_id_type=MESH,
        )

    def hand_off(k, _):
        s, g = replica_at(lax.rem(x + lax.rem(k // 8, 4), 4), lax.rem(z + lax.rem(k, 8), 8))
        t = lax.rem(y + k // 64, 4) * 2 + lax.rem(core + lax.rem(k // 32, 2), 2)
        page_copy(0, s, g, t).start()
        page_copy(1, s, g, t).start()
        return 0

    quarter = UNITS // 4
    lax.fori_loop(1, REPS, hand_off, 0)
    pl.semaphore_wait(ready, NTP - 1)
    lax.fori_loop(REPS, quarter, hand_off, 0)
    for kv in range(2):
        pltpu.make_async_copy(sendbuf.at[kv, me], pages[kv].at[me], page_recv.at[kv]).start()

    for copy in loads[2:]:
        copy.wait()
    shape = (STEPS * G * 16, 16 * CACHE)
    row = lax.broadcasted_iota(jnp.int32, shape, 0)
    col = lax.broadcasted_iota(jnp.int32, shape, 1)
    same_row = lax.rem(row, 16) == col // CACHE
    slot_of = lax.rem(col, CACHE)
    shape = (STEPS * G * 16, STEPS * 16)
    row = lax.broadcasted_iota(jnp.int32, shape, 0)
    col = lax.broadcasted_iota(jnp.int32, shape, 1)
    fresh_ok = jnp.logical_and(lax.rem(row, 16) == lax.rem(col, 16), col // 16 <= row // (G * 16))
    over_d = (((1,), (1,)), ((), ()))

    def decode(i, _):
        rows = pl.ds(pl.multiple_of(i * 16, 16), 16)
        query = jnp.concatenate(
            [dqbuf[s, rows, h * HD : (h + 1) * HD] for s in range(STEPS) for h in range(G)], axis=0
        )
        res_k = cbuf[0, rows].reshape(16 * CACHE, HD)
        res_v = cbuf[1, rows].reshape(16 * CACHE, HD)
        fresh_k = jnp.concatenate([nbuf[0, s, rows] for s in range(STEPS)], axis=0)
        fresh_v = jnp.concatenate([nbuf[1, s, rows] for s in range(STEPS)], axis=0)
        s1 = lax.dot_general(query, res_k, over_d, preferred_element_type=jnp.float32)
        s2 = lax.dot_general(query, fresh_k, over_d, preferred_element_type=jnp.float32)
        live = jnp.concatenate([lenbuf[rows]] * (STEPS * G), axis=0)
        ok = jnp.logical_and(same_row, slot_of < jnp.concatenate([live] * (16 * CACHE // HD), axis=1))
        s1 = jnp.where(ok, s1 * LOG2E_SCALE, MASKED)
        s2 = jnp.where(fresh_ok, s2 * LOG2E_SCALE, MASKED)
        peak = jnp.maximum(jnp.max(s1, axis=1, keepdims=True), jnp.max(s2, axis=1, keepdims=True))
        p1 = jnp.exp2(s1 - peak)
        p2 = jnp.exp2(s2 - peak)
        mass = jnp.sum(p1, axis=1, keepdims=True) + jnp.sum(p2, axis=1, keepdims=True)
        out = jnp.dot(p1.astype(jnp.bfloat16), res_v, preferred_element_type=jnp.float32)
        out = out + jnp.dot(p2.astype(jnp.bfloat16), fresh_v, preferred_element_type=jnp.float32)
        out = (out / mass).astype(jnp.bfloat16)
        for s in range(STEPS):
            for h in range(G):
                part = (s * G + h) * 16
                dec_out[0, s, rows, h * HD : (h + 1) * HD] = out[part : part + 16]
        return 0

    lax.fori_loop(0, ROWS // 16, decode, 0)

    top[...] = jnp.full_like(top, MASKED)
    total[...] = jnp.zeros_like(total)
    accum[...] = jnp.zeros_like(accum)
    shape = (ROW_TILE, CHIP_KEYS)
    ahead = lax.broadcasted_iota(jnp.int32, shape, 1) - lax.rem(
        lax.broadcasted_iota(jnp.int32, shape, 0), SPAN_DEV
    )
    ones = jnp.ones((CHIP_KEYS, HD), jnp.bfloat16)

    def attend(yy, reach, masked):
        allowed = ahead <= reach

        def head(g, _):
            lanes = pl.ds(pl.multiple_of(g * HD, HD), HD)
            keys = kbuf[pl.ds(yy * 2, 2), :, lanes].reshape(CHIP_KEYS, HD)
            values = vbuf[pl.ds(yy * 2, 2), :, lanes].reshape(CHIP_KEYS, HD)
            values = jnp.concatenate([values, ones], axis=1)
            parts = G * SPAN_DEV // ROW_TILE
            heads = ROW_TILE // SPAN_DEV

            def scores(part):
                query = jnp.concatenate(
                    [
                        qbuf[:, pl.ds(pl.multiple_of((g * G + part * heads + h) * HD, HD), HD)]
                        for h in range(heads)
                    ],
                    axis=0,
                )
                return lax.dot_general(query, keys, over_d, preferred_element_type=jnp.float32)

            s = scores(0)
            for part in range(parts):
                following = scores(part + 1) if part + 1 < parts else None
                where = pl.ds(part * ROW_TILE, ROW_TILE)
                s = s * LOG2E_SCALE
                if masked:
                    s = jnp.where(allowed, s, MASKED)
                old = top[g, where]
                new = jnp.maximum(old, jnp.max(s, axis=1, keepdims=True))
                weights = jnp.exp2(s - jnp.concatenate([new] * (CHIP_KEYS // HD), axis=1))
                fade = jnp.exp2(old - new)
                mix = jnp.dot(weights.astype(jnp.bfloat16), values, preferred_element_type=jnp.float32)
                top[g, where] = new
                accum[g, where] = accum[g, where] * fade + mix[:, :HD]
                total[g, where] = total[g, where] * fade + mix[:, HD:]
                s = following
            return 0

        lax.fori_loop(0, KVH, head, 0)

    own_k.wait()
    own_v.wait()

    def relay(j, kv):
        kv_arrival(chip_at(j) * 2 + core, kv).wait()
        kv_relayed(chip_at(j), kv).start()

    def step(j, _):
        here = chip_at(j)

        @pl.when(j == 1)
        def _():
            lax.fori_loop(quarter, 2 * quarter, hand_off, 0)

            @pl.when(uses(chip_at(2), y))
            def _():
                relay(2, 0)

            @pl.when(forwards(0))
            def _():
                kv_forward(0).start()

            @pl.when(uses(chip_at(1), y))
            def _():
                relay(1, 1)

            @pl.when(forwards(1))
            def _():
                kv_forward(1).start()

            @pl.when(uses(chip_at(1), y))
            def _():
                relay(1, 0)

            @pl.when(uses(chip_at(2), y))
            def _():
                relay(2, 1)

            lax.fori_loop(2 * quarter, UNITS, hand_off, 0)

        @pl.when(jnp.logical_and(j == 2, uses(chip_at(3), y)))
        def _():
            relay(3, 0)
            relay(3, 1)

        @pl.when(uses(here, y))
        def _():
            for kv in range(2):
                kv_arrival(here * 2 + 1 - core, kv).wait()
            reach = PRIOR + SPAN_DEV * tp - CHIP_KEYS * here

            @pl.when(reach < CHIP_KEYS - 1)
            def _():
                attend(here, reach, True)

            @pl.when(reach >= CHIP_KEYS - 1)
            def _():
                attend(here, reach, False)

        return 0

    lax.fori_loop(0, 4, step, 0)

    def finish(g, _):
        for h in range(G):
            where = pl.ds(h * SPAN_DEV, SPAN_DEV)
            lanes = pl.ds(pl.multiple_of((g * G + h) * HD, HD), HD)
            pre_out[0, :, lanes] = (accum[g, where] / total[g, where]).astype(jnp.bfloat16)
        return 0

    lax.fori_loop(0, KVH, finish, 0)

    for j in range(3):
        @pl.when(uses(y, chip_at(j)))
        def _():
            kv_direct(j, 0).wait_send()
            kv_direct(j, 1).wait_send()

    for kv in range(2):
        @pl.when(forwards(kv))
        def _():
            kv_forward(kv).wait_send()

    for j in range(1, 4):
        @pl.when(uses(chip_at(j), y))
        def _():
            kv_relayed(chip_at(j), 0).wait_send()
            kv_relayed(chip_at(j), 1).wait_send()

    some = pl.ds(0, UNITS - 1)
    for kv in range(2):
        pltpu.make_async_copy(sendbuf.at[kv, some], sendbuf.at[kv, some], page_send.at[kv]).wait()
        pltpu.make_async_copy(pages[kv], pages[kv], page_recv.at[kv]).wait()


def hand_on(*refs):
    held, results, sems = refs[:4], refs[4:8], refs[8]
    copies = [pltpu.make_async_copy(held[i], results[i], sems.at[i]) for i in range(4)]
    for copy in copies:
        copy.start()
    for copy in copies:
        copy.wait()


def body(
    pre_query,
    pre_keys,
    pre_values,
    dec_query,
    dec_new_keys,
    dec_new_values,
    cache_keys,
    cache_values,
    cache_lens,
    pool_keys,
    pool_values,
    block_owner,
    block_count,
):
    bf16, f32 = jnp.bfloat16, jnp.float32
    outside = pl.BlockSpec(memory_space=pltpu.HBM)
    on_chip = pl.BlockSpec(memory_space=pltpu.VMEM)
    pre_out, dec_out, pages_keys, pages_values = pl.pallas_call(
        kernel,
        out_shape=(
            pltpu.VMEM((1, SPAN_DEV, H * HD), bf16),
            pltpu.VMEM((1, STEPS, ROWS, G * HD), bf16),
            pltpu.VMEM((UNITS, CAP, BLOCK, HD), bf16),
            pltpu.VMEM((UNITS, CAP, BLOCK, HD), bf16),
        ),
        in_specs=[on_chip] * 3 + [outside] * 10,
        out_specs=(on_chip,) * 4,
        scratch_shapes=[
            pltpu.VMEM((SPAN_DEV, H * HD), bf16),
            pltpu.VMEM((NTP, KEY_DEV, KVH * HD), bf16),
            pltpu.VMEM((NTP, KEY_DEV, KVH * HD), bf16),
            pltpu.VMEM((2, 32, BLOCK, KVH * HD), bf16),
            pltpu.VMEM((2, UNITS, CAP, BLOCK, HD), bf16),
            pltpu.VMEM((KVH, G * SPAN_DEV, HD), f32),
            pltpu.VMEM((KVH, G * SPAN_DEV, HD), f32),
            pltpu.VMEM((KVH, G * SPAN_DEV, HD), f32),
            pltpu.VMEM((STEPS, ROWS, G * HD), bf16),
            pltpu.VMEM((2, STEPS, ROWS, HD), bf16),
            pltpu.VMEM((2, ROWS, CACHE, HD), bf16),
            pltpu.VMEM((ROWS, HD), jnp.int32),
            pltpu.VMEM((2, HD), jnp.int32),
            pltpu.SMEM((2, HD), jnp.int32),
            pltpu.SemaphoreType.REGULAR,
            pltpu.SemaphoreType.DMA((8,)),
            pltpu.SemaphoreType.DMA,
            pltpu.SemaphoreType.DMA((2,)),
            pltpu.SemaphoreType.DMA((2, 3)),
            pltpu.SemaphoreType.DMA((2,)),
            pltpu.SemaphoreType.DMA((2, 4)),
            pltpu.SemaphoreType.DMA((2, 8)),
            pltpu.SemaphoreType.DMA((2,)),
            pltpu.SemaphoreType.DMA((2,)),
        ],
        compiler_params=pltpu.CompilerParams(
            collective_id=0, has_side_effects=True, vmem_limit_bytes=48 * 2**20
        ),
    )(
        block_owner.reshape(1, -1),
        block_count.reshape(1, -1),
        cache_lens,
        pre_query,
        pre_keys,
        pre_values,
        dec_query,
        dec_new_keys,
        dec_new_values,
        cache_keys,
        cache_values,
        pool_keys,
        pool_values,
    )
    results = (pre_out, dec_out, pages_keys, pages_values)
    pre_out, dec_out, pages_keys, pages_values = pl.pallas_call(
        hand_on,
        out_shape=tuple(jax.ShapeDtypeStruct(v.shape, v.dtype) for v in results),
        in_specs=[on_chip] * 4,
        out_specs=(outside,) * 4,
        scratch_shapes=[pltpu.SemaphoreType.DMA((4,))],
        compiler_params=pltpu.CompilerParams(vmem_limit_bytes=2**20),
    )(*results)
    shape = (1, REPS, NTP, CAP, BLOCK, HD)
    return pre_out, dec_out, pages_keys.reshape(shape), pages_values.reshape(shape)


def solution(mesh):
    return jax.shard_map(
        body,
        mesh=mesh,
        in_specs=(
            P(("sec", "grp"), "tp", None),
            P(("sec", "grp"), "tp", None),
            P(("sec", "grp"), "tp", None),
            P(("sec", "grp"), None, None, "tp"),
            P(("sec", "grp"), None, None, "tp"),
            P(("sec", "grp"), None, None, "tp"),
            P(("sec", "grp"), None, None, "tp"),
            P(("sec", "grp"), None, None, "tp"),
            P(("sec", "grp"), None),
            P(("sec", "grp"), "tp", None, None, None),
            P(("sec", "grp"), "tp", None, None, None),
            P(("sec", "grp"), "tp", None, None),
            P(("sec", "grp"), "tp", None),
        ),
        out_specs=(
            P(("sec", "grp"), "tp", None),
            P(("sec", "grp"), None, None, "tp"),
            P(("sec", "grp"), None, None, None, None, "tp"),
            P(("sec", "grp"), None, None, None, None, "tp"),
        ),
        check_vma=False,
    )
```

```python
import jax
import jax.numpy as jnp
from jax import lax
from jax.experimental import pallas as pl
from jax.experimental.pallas import tpu as pltpu
from jax.sharding import PartitionSpec as P

H = 64
KVH = 8
HD = 128
G = 8
CAP = 2
BLOCK = 16
REPS = 32
NTP = 8
SPAN_DEV = 128
KEY_DEV = 256
CHIP_KEYS = 2 * KEY_DEV
PRIOR = 1024
ROWS = 64
STEPS = 2
CACHE = 16
UNITS = REPS * NTP
ROW_TILE = 256
LOG2E_SCALE = 1.4426950408889634 * HD**-0.5
MASKED = -1e30
MESH = pl.DeviceIdType.MESH


def position():
    sec, grp, tp = lax.axis_index("sec"), lax.axis_index("grp"), lax.axis_index("tp")
    return grp // 4, tp // 2, sec * 4 + lax.rem(grp, 4), lax.rem(tp, 2)


def replica_at(x, z):
    return z // 4, x * 4 + lax.rem(z, 4)


def kernel(
    owners,
    counts,
    lens,
    pre_q,
    pre_k,
    pre_v,
    dec_q,
    new_k,
    new_v,
    cache_k,
    cache_v,
    pool_k,
    pool_v,
    pre_out,
    dec_out,
    pages_k,
    pages_v,
    qbuf,
    kbuf,
    vbuf,
    poolbuf,
    sendbuf,
    top,
    total,
    accum,
    dqbuf,
    nbuf,
    cbuf,
    lenbuf,
    codebuf,
    table,
    ready,
    load_sem,
    table_sem,
    own_sem,
    kv_send,
    kv_onward,
    kv_relay,
    kv_recv,
    page_send,
    page_recv,
):
    x, y, z, core = position()
    sec, grp, tp = lax.axis_index("sec"), lax.axis_index("grp"), lax.axis_index("tp")
    me = (sec * 16 + grp) * NTP + tp
    other = y * 2 + 1 - core

    def shifted(k):
        return replica_at(lax.rem(x + k // 8, 4), lax.rem(z + lax.rem(k, 8), 8))

    def sibling(k):
        return lax.rem(tp + k, NTP)

    pages = (pages_k, pages_v)

    loads = [
        pltpu.make_async_copy(pool_k.at[0, 0], poolbuf.at[0], load_sem.at[0]),
        pltpu.make_async_copy(pool_v.at[0, 0], poolbuf.at[1], load_sem.at[1]),
        pltpu.make_async_copy(dec_q.at[0], dqbuf, load_sem.at[2]),
        pltpu.make_async_copy(new_k.at[0], nbuf.at[0], load_sem.at[3]),
        pltpu.make_async_copy(new_v.at[0], nbuf.at[1], load_sem.at[4]),
        pltpu.make_async_copy(cache_k.at[0], cbuf.at[0], load_sem.at[5]),
        pltpu.make_async_copy(cache_v.at[0], cbuf.at[1], load_sem.at[6]),
        pltpu.make_async_copy(pre_q.at[0], qbuf, load_sem.at[7]),
    ]
    own_k = pltpu.make_async_copy(pre_k.at[0], kbuf.at[tp], own_sem.at[0])
    own_v = pltpu.make_async_copy(pre_v.at[0], vbuf.at[tp], own_sem.at[1])

    loads[0].start()
    loads[1].start()

    barrier = pltpu.get_barrier_semaphore()

    def greet_replicas(k, _):
        s, g = shifted(k)
        pl.semaphore_signal(barrier, inc=1, device_id=(s, g, tp), device_id_type=MESH)
        return 0

    def greet_siblings(k, _):
        pl.semaphore_signal(barrier, inc=1, device_id=(sec, grp, sibling(k)), device_id_type=MESH)
        return 0

    lax.fori_loop(1, REPS, greet_replicas, 0, unroll=True)
    lax.fori_loop(1, NTP, greet_siblings, 0, unroll=True)
    for copy in loads[2:]:
        copy.start()
    own_k.start()
    own_v.start()

    pool_len = owners.shape[1]
    first = lax.broadcasted_iota(jnp.int32, (pool_len, pool_len), 0)
    second = lax.broadcasted_iota(jnp.int32, (pool_len, pool_len), 1)
    same = first == second
    owner_row = owners[...]
    owner_col = jnp.sum(jnp.where(same, owner_row, 0), axis=1, keepdims=True)
    count_col = jnp.sum(jnp.where(same, counts[...], 0), axis=1, keepdims=True)
    earlier = jnp.logical_and(owner_row == owner_col, second < first)
    slot_col = jnp.sum(jnp.where(earlier, 1, 0), axis=1, keepdims=True)
    chosen = owner_col * CAP + slot_col == lax.broadcasted_iota(jnp.int32, (pool_len, 128), 1)
    block_col = lax.broadcasted_iota(jnp.int32, (pool_len, 128), 0)
    codebuf[0:1] = jnp.sum(jnp.where(chosen, block_col, 0), axis=0, keepdims=True)
    codebuf[1:2] = jnp.sum(jnp.where(chosen, count_col, 0), axis=0, keepdims=True)
    to_scalars = pltpu.make_async_copy(codebuf, table, table_sem)
    to_scalars.start()
    first = lax.broadcasted_iota(jnp.int32, (ROWS, ROWS), 0)
    second = lax.broadcasted_iota(jnp.int32, (ROWS, ROWS), 1)
    len_col = jnp.sum(jnp.where(first == second, lens[...], 0), axis=1, keepdims=True)
    lenbuf[...] = jnp.broadcast_to(len_col, lenbuf.shape)
    to_scalars.wait()

    loads[0].wait()
    loads[1].wait()
    token = lax.broadcasted_iota(jnp.int32, (BLOCK, HD), 0)
    blank = jnp.zeros((BLOCK, HD), jnp.bfloat16)

    def pack(owner):
        for slot in range(CAP):
            block = table[0, owner * CAP + slot]
            live = table[1, owner * CAP + slot]
            keep = token < live
            for kv in range(2):
                rows = poolbuf[kv, block]
                for t in range(NTP):
                    part = rows[:, t * HD : (t + 1) * HD]
                    sendbuf[kv, owner * NTP + t, slot] = jnp.where(keep, part, blank)

    def pack_group(group):
        xx = lax.rem(x + group, 4)

        def one(zz, _):
            pack((zz // 4) * 16 + xx * 4 + lax.rem(zz, 4))
            return 0

        lax.fori_loop(0, 8, one, 0)

    pack_group(0)
    pl.semaphore_wait(barrier, REPS - 1 + NTP - 1)

    def vouch(k, _):
        pl.semaphore_signal(ready, inc=1, device_id=(sec, grp, sibling(k)), device_id_type=MESH)
        return 0

    lax.fori_loop(1, NTP, vouch, 0)

    def chip_at(j):
        return lax.rem(y + jnp.where(j == 0, 0, jnp.where(j == 1, 1, jnp.where(j == 2, 3, 2))), 4)

    def uses(holder, user):
        return jnp.logical_or(holder < 3, user >= 2)

    def kv_direct(j, kv):
        source = (pre_k, pre_v)[kv]
        buf = (kbuf, vbuf)[kv]
        peer = other if j == 0 else chip_at(j) * 2 + core
        return pltpu.make_async_remote_copy(
            src_ref=source.at[0],
            dst_ref=buf.at[tp],
            send_sem=kv_send.at[kv, j],
            recv_sem=kv_recv.at[kv, tp],
            device_id=(sec, grp, peer),
            device_id_type=MESH,
        )

    def kv_forward(kv):
        buf = (kbuf, vbuf)[kv]
        source, target = (chip_at(2), chip_at(1)) if kv == 0 else (chip_at(1), chip_at(2))
        chunk = source * 2 + core
        return pltpu.make_async_remote_copy(
            src_ref=buf.at[chunk],
            dst_ref=buf.at[chunk],
            send_sem=kv_onward.at[kv],
            recv_sem=kv_recv.at[kv, chunk],
            device_id=(sec, grp, target * 2 + core),
            device_id_type=MESH,
        )

    def forwards(kv):
        source, target = (chip_at(2), chip_at(1)) if kv == 0 else (chip_at(1), chip_at(2))
        return jnp.logical_and(uses(source, y), uses(source, target))

    def kv_relayed(yy, kv):
        buf = (kbuf, vbuf)[kv]
        chunk = yy * 2 + core
        return pltpu.make_async_remote_copy(
            src_ref=buf.at[chunk],
            dst_ref=buf.at[chunk],
            send_sem=kv_relay.at[kv, yy],
            recv_sem=kv_recv.at[kv, chunk],
            device_id=(sec, grp, other),
            device_id_type=MESH,
        )

    def kv_arrival(chunk, kv):
        buf = (kbuf, vbuf)[kv]
        return pltpu.make_async_copy(buf.at[chunk], buf.at[chunk], kv_recv.at[kv, chunk])

    for j in (1, 2, 0):
        @pl.when(uses(y, chip_at(j)))
        def _():
            kv_direct(j, 0).start()
            kv_direct(j, 1).start()


    def page_copy(kv, s, g, t):
        return pltpu.make_async_remote_copy(
            src_ref=sendbuf.at[kv, (s * 16 + g) * NTP + t],
            dst_ref=pages[kv].at[me],
            send_sem=page_send.at[kv],
            recv_sem=page_recv.at[kv],
            device_id=(s, g, t),
            device_id_type=MESH,
        )

    def hand_off(group, first=0):
        xx = lax.rem(x + lax.rem(group, 4), 4)
        t = lax.rem(y + group // 8, 4) * 2 + lax.rem(core + lax.rem(group // 4, 2), 2)
        for dz in range(first, 8):
            s, g = replica_at(xx, lax.rem(z + dz, 8))
            page_copy(0, s, g, t).start()
            page_copy(1, s, g, t).start()

    def cross(turn, _):
        way = lax.rem(turn, 3)
        dy = jnp.where(way == 0, 1, jnp.where(way == 1, 3, 2))
        hand_off(dy * 8 + turn // 3)
        return 0

    def hand_off_groups(begin, end):
        def one(group, _):
            hand_off(group)
            return 0

        lax.fori_loop(begin, end, one, 0)

    hand_off(0, 1)

    def first_round(group, _):
        pack_group(group)
        hand_off(group)
        return 0

    lax.fori_loop(1, 4, first_round, 0)
    pl.semaphore_wait(ready, NTP - 1)
    hand_off_groups(4, 8)
    for kv in range(2):
        pltpu.make_async_copy(sendbuf.at[kv, me], pages[kv].at[me], page_recv.at[kv]).start()

    for copy in loads[2:]:
        copy.wait()
    shape = (STEPS * G * 16, 16 * CACHE)
    row = lax.broadcasted_iota(jnp.int32, shape, 0)
    col = lax.broadcasted_iota(jnp.int32, shape, 1)
    same_row = lax.rem(row, 16) == col // CACHE
    slot_of = lax.rem(col, CACHE)
    shape = (STEPS * G * 16, STEPS * 16)
    row = lax.broadcasted_iota(jnp.int32, shape, 0)
    col = lax.broadcasted_iota(jnp.int32, shape, 1)
    fresh_ok = jnp.logical_and(lax.rem(row, 16) == lax.rem(col, 16), col // 16 <= row // (G * 16))
    over_d = (((1,), (1,)), ((), ()))

    def decode(i, _):
        rows = pl.ds(pl.multiple_of(i * 16, 16), 16)
        query = jnp.concatenate(
            [dqbuf[s, rows, h * HD : (h + 1) * HD] for s in range(STEPS) for h in range(G)], axis=0
        )
        res_k = cbuf[0, rows].reshape(16 * CACHE, HD)
        res_v = cbuf[1, rows].reshape(16 * CACHE, HD)
        fresh_k = jnp.concatenate([nbuf[0, s, rows] for s in range(STEPS)], axis=0)
        fresh_v = jnp.concatenate([nbuf[1, s, rows] for s in range(STEPS)], axis=0)
        s1 = lax.dot_general(query, res_k, over_d, preferred_element_type=jnp.float32)
        s2 = lax.dot_general(query, fresh_k, over_d, preferred_element_type=jnp.float32)
        live = jnp.concatenate([lenbuf[rows]] * (STEPS * G), axis=0)
        ok = jnp.logical_and(same_row, slot_of < jnp.concatenate([live] * (16 * CACHE // HD), axis=1))
        s1 = jnp.where(ok, s1 * LOG2E_SCALE, MASKED)
        s2 = jnp.where(fresh_ok, s2 * LOG2E_SCALE, MASKED)
        peak = jnp.maximum(jnp.max(s1, axis=1, keepdims=True), jnp.max(s2, axis=1, keepdims=True))
        p1 = jnp.exp2(s1 - peak)
        p2 = jnp.exp2(s2 - peak)
        mass = jnp.sum(p1, axis=1, keepdims=True) + jnp.sum(p2, axis=1, keepdims=True)
        out = jnp.dot(p1.astype(jnp.bfloat16), res_v, preferred_element_type=jnp.float32)
        out = out + jnp.dot(p2.astype(jnp.bfloat16), fresh_v, preferred_element_type=jnp.float32)
        out = (out / mass).astype(jnp.bfloat16)
        for s in range(STEPS):
            for h in range(G):
                part = (s * G + h) * 16
                dec_out[0, s, rows, h * HD : (h + 1) * HD] = out[part : part + 16]
        return 0

    lax.fori_loop(0, ROWS // 16, decode, 0)

    top[...] = jnp.full_like(top, MASKED)
    total[...] = jnp.zeros_like(total)
    accum[...] = jnp.zeros_like(accum)
    shape = (ROW_TILE, CHIP_KEYS)
    ahead = lax.broadcasted_iota(jnp.int32, shape, 1) - lax.rem(
        lax.broadcasted_iota(jnp.int32, shape, 0), SPAN_DEV
    )
    ones = jnp.ones((CHIP_KEYS, HD), jnp.bfloat16)

    def attend(yy, reach, masked):
        allowed = ahead <= reach

        def head(g, _):
            lanes = pl.ds(pl.multiple_of(g * HD, HD), HD)
            keys = kbuf[pl.ds(yy * 2, 2), :, lanes].reshape(CHIP_KEYS, HD)
            values = vbuf[pl.ds(yy * 2, 2), :, lanes].reshape(CHIP_KEYS, HD)
            values = jnp.concatenate([values, ones], axis=1)
            parts = G * SPAN_DEV // ROW_TILE
            heads = ROW_TILE // SPAN_DEV

            def scores(part):
                query = jnp.concatenate(
                    [
                        qbuf[:, pl.ds(pl.multiple_of((g * G + part * heads + h) * HD, HD), HD)]
                        for h in range(heads)
                    ],
                    axis=0,
                )
                return lax.dot_general(query, keys, over_d, preferred_element_type=jnp.float32)

            s = scores(0)
            for part in range(parts):
                following = scores(part + 1) if part + 1 < parts else None
                where = pl.ds(part * ROW_TILE, ROW_TILE)
                s = s * LOG2E_SCALE
                if masked:
                    s = jnp.where(allowed, s, MASKED)
                old = top[g, where]
                new = jnp.maximum(old, jnp.max(s, axis=1, keepdims=True))
                weights = jnp.exp2(s - jnp.concatenate([new] * (CHIP_KEYS // HD), axis=1))
                fade = jnp.exp2(old - new)
                mix = jnp.dot(weights.astype(jnp.bfloat16), values, preferred_element_type=jnp.float32)
                top[g, where] = new
                accum[g, where] = accum[g, where] * fade + mix[:, :HD]
                total[g, where] = total[g, where] * fade + mix[:, HD:]
                s = following
            return 0

        lax.fori_loop(0, KVH, head, 0)

    own_k.wait()
    own_v.wait()

    def relay(j, kv):
        kv_arrival(chip_at(j) * 2 + core, kv).wait()
        kv_relayed(chip_at(j), kv).start()

    def step(j, _):
        here = chip_at(j)

        @pl.when(j == 1)
        def _():
            lax.fori_loop(0, 8, cross, 0)

            @pl.when(uses(chip_at(2), y))
            def _():
                relay(2, 0)

            @pl.when(forwards(0))
            def _():
                kv_forward(0).start()

            @pl.when(uses(chip_at(1), y))
            def _():
                relay(1, 1)

            @pl.when(forwards(1))
            def _():
                kv_forward(1).start()

            @pl.when(uses(chip_at(1), y))
            def _():
                relay(1, 0)

            @pl.when(uses(chip_at(2), y))
            def _():
                relay(2, 1)

            lax.fori_loop(8, 24, cross, 0)

        @pl.when(jnp.logical_and(j == 2, uses(chip_at(3), y)))
        def _():
            relay(3, 0)
            relay(3, 1)

        @pl.when(uses(here, y))
        def _():
            for kv in range(2):
                kv_arrival(here * 2 + 1 - core, kv).wait()
            reach = PRIOR + SPAN_DEV * tp - CHIP_KEYS * here

            @pl.when(reach < CHIP_KEYS - 1)
            def _():
                attend(here, reach, True)

            @pl.when(reach >= CHIP_KEYS - 1)
            def _():
                attend(here, reach, False)

        return 0

    lax.fori_loop(0, 4, step, 0)

    def finish(g, _):
        for h in range(G):
            where = pl.ds(h * SPAN_DEV, SPAN_DEV)
            lanes = pl.ds(pl.multiple_of((g * G + h) * HD, HD), HD)
            pre_out[0, :, lanes] = (accum[g, where] / total[g, where]).astype(jnp.bfloat16)
        return 0

    lax.fori_loop(0, KVH, finish, 0)

    for j in range(3):
        @pl.when(uses(y, chip_at(j)))
        def _():
            kv_direct(j, 0).wait_send()
            kv_direct(j, 1).wait_send()

    for kv in range(2):
        @pl.when(forwards(kv))
        def _():
            kv_forward(kv).wait_send()

    for j in range(1, 4):
        @pl.when(uses(chip_at(j), y))
        def _():
            kv_relayed(chip_at(j), 0).wait_send()
            kv_relayed(chip_at(j), 1).wait_send()

    some = pl.ds(0, UNITS - 1)
    for kv in range(2):
        pltpu.make_async_copy(sendbuf.at[kv, some], sendbuf.at[kv, some], page_send.at[kv]).wait()
        pltpu.make_async_copy(pages[kv], pages[kv], page_recv.at[kv]).wait()


def hand_on(*refs):
    held, results, sems = refs[:4], refs[4:8], refs[8]
    pieces = [(0, 1, pl.ds(i * 32, 32)) for i in range(4)]
    pieces += [(ref, 0, pl.ds(i * 64, 64)) for ref in (2, 3) for i in range(4)]
    copies = [pltpu.make_async_copy(held[1], results[1], sems.at[0])]
    for i, (ref, axis, part) in enumerate(pieces):
        where = (0, part) if axis else (part,)
        copies.append(pltpu.make_async_copy(held[ref].at[where], results[ref].at[where], sems.at[i + 1]))
    for copy in copies:
        copy.start()
    for copy in copies:
        copy.wait()


def body(
    pre_query,
    pre_keys,
    pre_values,
    dec_query,
    dec_new_keys,
    dec_new_values,
    cache_keys,
    cache_values,
    cache_lens,
    pool_keys,
    pool_values,
    block_owner,
    block_count,
):
    bf16, f32 = jnp.bfloat16, jnp.float32
    outside = pl.BlockSpec(memory_space=pltpu.HBM)
    on_chip = pl.BlockSpec(memory_space=pltpu.VMEM)
    pre_out, dec_out, pages_keys, pages_values = pl.pallas_call(
        kernel,
        out_shape=(
            pltpu.VMEM((1, SPAN_DEV, H * HD), bf16),
            pltpu.VMEM((1, STEPS, ROWS, G * HD), bf16),
            pltpu.VMEM((UNITS, CAP, BLOCK, HD), bf16),
            pltpu.VMEM((UNITS, CAP, BLOCK, HD), bf16),
        ),
        in_specs=[on_chip] * 3 + [outside] * 10,
        out_specs=(on_chip,) * 4,
        scratch_shapes=[
            pltpu.VMEM((SPAN_DEV, H * HD), bf16),
            pltpu.VMEM((NTP, KEY_DEV, KVH * HD), bf16),
            pltpu.VMEM((NTP, KEY_DEV, KVH * HD), bf16),
            pltpu.VMEM((2, 32, BLOCK, KVH * HD), bf16),
            pltpu.VMEM((2, UNITS, CAP, BLOCK, HD), bf16),
            pltpu.VMEM((KVH, G * SPAN_DEV, HD), f32),
            pltpu.VMEM((KVH, G * SPAN_DEV, HD), f32),
            pltpu.VMEM((KVH, G * SPAN_DEV, HD), f32),
            pltpu.VMEM((STEPS, ROWS, G * HD), bf16),
            pltpu.VMEM((2, STEPS, ROWS, HD), bf16),
            pltpu.VMEM((2, ROWS, CACHE, HD), bf16),
            pltpu.VMEM((ROWS, HD), jnp.int32),
            pltpu.VMEM((2, HD), jnp.int32),
            pltpu.SMEM((2, HD), jnp.int32),
            pltpu.SemaphoreType.REGULAR,
            pltpu.SemaphoreType.DMA((8,)),
            pltpu.SemaphoreType.DMA,
            pltpu.SemaphoreType.DMA((2,)),
            pltpu.SemaphoreType.DMA((2, 3)),
            pltpu.SemaphoreType.DMA((2,)),
            pltpu.SemaphoreType.DMA((2, 4)),
            pltpu.SemaphoreType.DMA((2, 8)),
            pltpu.SemaphoreType.DMA((2,)),
            pltpu.SemaphoreType.DMA((2,)),
        ],
        compiler_params=pltpu.CompilerParams(
            collective_id=0, has_side_effects=True, vmem_limit_bytes=48 * 2**20
        ),
    )(
        block_owner.reshape(1, -1),
        block_count.reshape(1, -1),
        cache_lens,
        pre_query,
        pre_keys,
        pre_values,
        dec_query,
        dec_new_keys,
        dec_new_values,
        cache_keys,
        cache_values,
        pool_keys,
        pool_values,
    )
    results = (pre_out, dec_out, pages_keys, pages_values)
    pre_out, dec_out, pages_keys, pages_values = pl.pallas_call(
        hand_on,
        out_shape=tuple(jax.ShapeDtypeStruct(v.shape, v.dtype) for v in results),
        in_specs=[on_chip] * 4,
        out_specs=(outside,) * 4,
        scratch_shapes=[pltpu.SemaphoreType.DMA((13,))],
        compiler_params=pltpu.CompilerParams(vmem_limit_bytes=2**20),
    )(*results)
    shape = (1, REPS, NTP, CAP, BLOCK, HD)
    return pre_out, dec_out, pages_keys.reshape(shape), pages_values.reshape(shape)


def solution(mesh):
    return jax.shard_map(
        body,
        mesh=mesh,
        in_specs=(
            P(("sec", "grp"), "tp", None),
            P(("sec", "grp"), "tp", None),
            P(("sec", "grp"), "tp", None),
            P(("sec", "grp"), None, None, "tp"),
            P(("sec", "grp"), None, None, "tp"),
            P(("sec", "grp"), None, None, "tp"),
            P(("sec", "grp"), None, None, "tp"),
            P(("sec", "grp"), None, None, "tp"),
            P(("sec", "grp"), None),
            P(("sec", "grp"), "tp", None, None, None),
            P(("sec", "grp"), "tp", None, None, None),
            P(("sec", "grp"), "tp", None, None),
            P(("sec", "grp"), "tp", None),
        ),
        out_specs=(
            P(("sec", "grp"), "tp", None),
            P(("sec", "grp"), None, None, "tp"),
            P(("sec", "grp"), None, None, None, None, "tp"),
            P(("sec", "grp"), None, None, None, None, "tp"),
        ),
        check_vma=False,
    )
```
